32 devices in a mesh: lon: 8 (over z, core), lat: 4 (over y, x).
Axes of the slice: x: 2, y: 2, z: 4, core: 2. Of those that a mesh axis runs over, the one named last changes fastest.
Arguments:
- zonal_current: float32 [32, 256, 1024], P(None, 'lat', 'lon'), may hold values from -6 to 6
- meridional_current: float32 [32, 256, 1024], P(None, 'lat', 'lon'), may hold values from -6 to 6
- warmth_anomaly: float32 [32, 256, 1024], P(None, 'lat', 'lon'), may hold values from -6 to 6
- brine_anomaly: float32 [32, 256, 1024], P(None, 'lat', 'lon'), may hold values from -6 to 6
- marine_indicator: int32 [256, 1024], P('lat', 'lon'), may hold values 0 or 1
- retained_tile_indicator: int32 [16, 64], P('lat', 'lon'), may hold values 0 or 1
- seabed_thickness: float32 [256, 1024], P('lat', 'lon'), may hold values from 0.25 to 2.5
- elevation_pivot_entry: float32 [256, 1024], P('lat', 'lon'), may hold values from 0.1 to 1
Outputs:
- zonal_next: float32 [32, 256, 1024], P(None, 'lat', 'lon')
- meridional_next: float32 [32, 256, 1024], P(None, 'lat', 'lon')
- temperature_next: float32 [32, 256, 1024], P(None, 'lat', 'lon')
- salinity_next: float32 [32, 256, 1024], P(None, 'lat', 'lon')
- surface_pressure: float32 [256, 1024], P('lat', 'lon')
- pressure_residual: float32 [256, 1024], P('lat', 'lon')
The draws below stay inside these ranges and needn't reach their ends.
All inputs are finite; a program needn't handle non-finite values. No bound on the sum of `marine_indicator` or of `retained_tile_indicator` on one device may be relied on, other than what follows from the above.
Results may differ from the reference program's by a relative error of at most 0.0003.
Values sent between devices are 32-bit elements; how exact they have to be, the bound alone decides.
A program may use at most 128 MiB of HBM per device.

```python
import math
import jax
import jax.numpy as jnp
from jax import lax

VERTICAL_TIERS = 32
BLK = 16
ITERS = 3
PARALLEL_POINTS = 1024
MERIDIAN_POINTS = 256
NBX = 64
NBY = 16


def set_ends(drawn, stream_key, low, top_value):
    shape = drawn.shape
    spot = [jax.random.randint(jax.random.fold_in(stream_key, axis), (), 0, shape[axis]) for axis in range(len(shape))]
    drawn = drawn.at[tuple(spot)].set(low)
    longest = shape.index(max(shape))
    spot[longest] = (spot[longest] + 1) % shape[longest]
    return drawn.at[tuple(spot)].set(top_value)


def shard_levels(own_key, dims, cuts, low, largest):
    loudness = 1.0
    for axis_at, blocks in cuts:
        heights = jax.random.uniform(jax.random.fold_in(jax.random.fold_in(own_key, 6), axis_at), (blocks,), jnp.float32, low / len(cuts), largest / len(cuts))
        loudness = loudness * jnp.repeat(jnp.exp(heights), dims[axis_at] // blocks).reshape((-1,) + (1,) * (len(dims) - 1 - axis_at))
    return loudness


def scatter_about(rng, dims, deviation, reach, pieces=(), kind=jnp.bfloat16):
    array = jax.random.normal(rng, dims, jnp.float32) * deviation
    if len(pieces) > 0:
        array = shard_levels(rng, dims, pieces, -0.22, 0.18) * array
    return jnp.clip(array, min=-reach, max=reach).astype(kind)


def setup_inputs(seed: int = 0) -> dict:
    streams_of = jax.random.split(jax.random.key(seed), 9)
    return {
        "zonal_current": scatter_about(streams_of[0], (VERTICAL_TIERS, MERIDIAN_POINTS, PARALLEL_POINTS), 1.0, 6.0, ((1, 4), (2, 8)), jnp.float32),
        "meridional_current": scatter_about(streams_of[1], (VERTICAL_TIERS, MERIDIAN_POINTS, PARALLEL_POINTS), 1.0, 6.0, ((1, 4), (2, 8)), jnp.float32),
        "warmth_anomaly": scatter_about(streams_of[2], (VERTICAL_TIERS, MERIDIAN_POINTS, PARALLEL_POINTS), 1.0, 6.0, ((1, 4), (2, 8)), jnp.float32),
        "brine_anomaly": scatter_about(streams_of[3], (VERTICAL_TIERS, MERIDIAN_POINTS, PARALLEL_POINTS), 1.0, 6.0, ((1, 4), (2, 8)), jnp.float32),
        "marine_indicator": set_ends((jax.random.randint(streams_of[4], (MERIDIAN_POINTS, PARALLEL_POINTS), 0, 4) < 3).astype(jnp.int32), jax.random.fold_in(streams_of[4], 1), 0, 1),
        "retained_tile_indicator": set_ends((jax.random.randint(streams_of[5], (NBY, NBX), 0, 8) < 7).astype(jnp.int32), jax.random.fold_in(streams_of[5], 1), 0, 1),
        "seabed_thickness": jnp.clip(jnp.exp(math.log(2.5) - 2.3025851 * jax.random.uniform(streams_of[6], (MERIDIAN_POINTS, PARALLEL_POINTS), jnp.float32) ** shard_levels(streams_of[6], (MERIDIAN_POINTS, PARALLEL_POINTS), ((0, 4), (1, 8)), -0.2, 0.2)), 0.25, 2.5),
        "elevation_pivot_entry": jnp.clip(jnp.exp(math.log(1.0) - 2.3025851 * jax.random.uniform(streams_of[7], (MERIDIAN_POINTS, PARALLEL_POINTS), jnp.float32) ** shard_levels(streams_of[7], (MERIDIAN_POINTS, PARALLEL_POINTS), ((0, 4), (1, 8)), -0.2, 0.2)), 0.1, 1.0),
    }


time_step = 0.1
viscosity = 0.2
diffusivity = 0.15
thermal = 0.2
haline = 0.8
source_gain = 8.0


def beside_all(field, parity):
    east_cell = jnp.roll(field, -1, axis=-1)
    west_cell = jnp.roll(field, 1, axis=-1)
    north_cell = jnp.concatenate([field[..., 1:, :], parity * field[..., -1:, ::-1]], axis=-2)
    south_cell = jnp.concatenate([jnp.zeros_like(field[..., :1, :]), field[..., :-1, :]], axis=-2)
    return east_cell, west_cell, north_cell, south_cell


def laplace(field, near):
    return near[0] + near[1] + near[2] + near[3] - 4.0 * field


def reference(zonal_current, meridional_current, warmth_anomaly, brine_anomaly, marine_indicator, retained_tile_indicator, seabed_thickness, elevation_pivot_entry):
    marine_snapshot = marine_indicator.astype(jnp.float32)
    rows_global = jnp.arange(MERIDIAN_POINTS).astype(jnp.float32)
    coriolis = (2.0 * (rows_global + 0.5) / MERIDIAN_POINTS - 1.0)[:, None]

    def march_single_tier(iterate_carry, inputs):
        pressure, zonal_sum, merid_sum = iterate_carry
        zonal = inputs[0] * marine_snapshot
        merid = inputs[1] * marine_snapshot
        enthalpy_content = inputs[2] * marine_snapshot
        salt = inputs[3] * marine_snapshot
        pressure = pressure + (haline * salt - thermal * enthalpy_content)
        near_p = beside_all(pressure, 1.0)
        near_u = beside_all(zonal, -1.0)
        near_v = beside_all(merid, -1.0)
        near_t = beside_all(enthalpy_content, 1.0)
        near_s = beside_all(salt, 1.0)
        zonal_new = marine_snapshot * (zonal + time_step * (coriolis * merid - 0.5 * (near_p[0] - near_p[1]) + viscosity * laplace(zonal, near_u)))
        merid_new = marine_snapshot * (merid + time_step * (-coriolis * zonal - 0.5 * (near_p[2] - near_p[3]) + viscosity * laplace(merid, near_v)))
        outs = []
        for tracer, near_q in ((enthalpy_content, near_t), (salt, near_s)):
            flux = 0.5 * (near_u[0] * near_q[0] - near_u[1] * near_q[1] + near_v[2] * near_q[2] - near_v[3] * near_q[3])
            outs.append(marine_snapshot * (tracer + time_step * (-flux + diffusivity * laplace(tracer, near_q))))
        return (pressure, zonal_sum + zonal_new, merid_sum + merid_new), (zonal_new, merid_new, outs[0], outs[1])

    blank_tier = jnp.zeros((MERIDIAN_POINTS, PARALLEL_POINTS), jnp.float32)
    iterate_carry, tier_sequence = lax.scan(march_single_tier, (blank_tier, blank_tier, blank_tier), (zonal_current, meridional_current, warmth_anomaly, brine_anomaly))
    zonal_mean = iterate_carry[1] / VERTICAL_TIERS
    merid_mean = iterate_carry[2] / VERTICAL_TIERS
    kept = jnp.repeat(jnp.repeat(retained_tile_indicator.astype(jnp.float32), BLK, axis=0), BLK, axis=1)
    open_cells = marine_snapshot * kept
    column = seabed_thickness * open_cells
    near_um = beside_all(zonal_mean, -1.0)
    near_vm = beside_all(merid_mean, -1.0)
    rhs = -source_gain * open_cells * 0.5 * (near_um[0] - near_um[1] + near_vm[2] - near_vm[3])
    near_c = beside_all(column, 1.0)
    weights = [0.5 * (column + near_c[0]), 0.5 * (column + near_c[1]), 0.5 * (column + near_c[2]), 0.5 * (column + near_c[3])]
    diag = elevation_pivot_entry + weights[0] + weights[1] + weights[2] + weights[3]

    def apply(vector):
        near_x = beside_all(vector, 1.0)
        return open_cells * (diag * vector - weights[0] * near_x[0] - weights[1] * near_x[1] - weights[2] * near_x[2] - weights[3] * near_x[3])

    solution = jnp.zeros_like(rhs)
    residual = rhs
    precond = residual / diag
    direction = precond
    product_now = jnp.sum(residual * precond)
    for step in range(ITERS):
        image = apply(direction)
        alpha = product_now / jnp.sum(direction * image)
        solution = solution + alpha * direction
        residual = residual - alpha * image
        precond = residual / diag
        product_next = jnp.sum(residual * precond)
        direction = precond + (product_next / product_now) * direction
        product_now = product_next
    return tier_sequence[0], tier_sequence[1], tier_sequence[2], tier_sequence[3], solution, residual
```

```python
import functools

import jax
import jax.numpy as jnp
from jax import lax
from jax.experimental import pallas as pl
from jax.experimental.pallas import tpu as pltpu
from jax.sharding import PartitionSpec as P

BLK = 16
ITERS = 3

time_step = 0.1
viscosity = 0.2
diffusivity = 0.15
thermal = 0.2
haline = 0.8
source_gain = 8.0

NF = 4
NA = 6
STRIP = 16
S8 = 8
QROWS = 16
PAD = 8


def reverse_lanes(x):
    index = x.shape[-1] - 1 - lax.broadcasted_iota(jnp.int32, x.shape, x.ndim - 1)
    return jnp.take_along_axis(x, index, axis=x.ndim - 1, mode="promise_in_bounds")


def roll(x, shift, axis):
    return pltpu.roll(x, shift % x.shape[axis], axis)


def near(x):
    return roll(x, -1, 1), roll(x, 1, 1), roll(x, -1, 0), roll(x, 1, 0)


def surface_kernel(
    u_ref, v_ref, t_ref, s_ref, marine_ref, kept_ref, depth_ref, elev_ref,
    edge_ref, rows_ref, sol_ref, res_ref,
    held, send_e, send_w, send_v, recv_e, recv_w, recv_v, recv_c, ext,
    part_lon, part_lat, load_sem, send_sem, recv_sem, lon_send, lon_recv, lat_send, lat_recv,
):
    n_lon, n_lat = lax.axis_size("lon"), lax.axis_size("lat")
    lon, lat = lax.axis_index("lon"), lax.axis_index("lat")
    levels, height, breadth = u_ref.shape
    last = lat == n_lat - 1
    east, west = lax.rem(lon + 1, n_lon), lax.rem(lon + n_lon - 1, n_lon)
    mirror = n_lon - 1 - lon

    fields = (u_ref, v_ref, t_ref, s_ref)
    quarters = height // QROWS
    loads = []
    for q in range(quarters):
        row = []
        for f in range(NF):
            copy = pltpu.make_async_copy(
                fields[f].at[:, pl.ds(q * QROWS, QROWS), :],
                held.at[f, :, pl.ds(q * QROWS, QROWS), :],
                load_sem.at[q, f],
            )
            copy.start()
            row.append(copy)
        loads.append(row)

    barrier = pltpu.get_barrier_semaphore()

    def greet(a, b):
        pl.semaphore_signal(
            barrier, inc=1, device_id={"lon": a, "lat": b}, device_id_type=pl.DeviceIdType.MESH
        )

    for o in range(1, n_lon):
        greet(lax.rem(lon + o, n_lon), lat)
    for o in range(1, n_lat):
        greet(lon, lax.rem(lat + o, n_lat))

    @pl.when(lat > 0)
    def _():
        greet(east, lat - 1)
        greet(west, lat - 1)

    @pl.when(lat < n_lat - 1)
    def _():
        greet(east, lat + 1)
        greet(west, lat + 1)

    lane = lax.broadcasted_iota(jnp.int32, (height, breadth), 1)
    ocean = marine_ref[...].astype(jnp.float32)
    bands = []
    lane_band = lax.broadcasted_iota(jnp.int32, (BLK, breadth), 1) // BLK
    for jb in range(height // BLK):
        band = jnp.zeros((BLK, breadth), jnp.float32)
        for ib in range(breadth // BLK):
            band = jnp.where(lane_band == ib, kept_ref[jb, ib].astype(jnp.float32), band)
        bands.append(band)
    kept = jnp.concatenate(bands, axis=0)
    ext[0, PAD : PAD + height, 0:breadth] = ocean
    ext[1, PAD : PAD + height, 0:breadth] = depth_ref[...] * (ocean * kept)
    ext[2, PAD : PAD + height, 0:breadth] = elev_ref[...]

    lane_q = lax.broadcasted_iota(jnp.int32, (QROWS, breadth), 1)
    even_q = lax.rem(lane_q, 2) == 0
    for q in range(quarters):
        for copy in loads[q]:
            copy.wait()
        r0 = q * QROWS

        def level_step(l, carry, r0=r0, q=q):
            even, odd, su, sv, sp = carry
            weight = (levels - l).astype(jnp.float32) * (1.0 / levels)
            x = [held[f, l, r0 : r0 + QROWS, :] for f in range(NF)]
            for f in range(NF):
                k = NF * l + f
                turned = pltpu.roll(x[f], k, 1)
                before = jnp.where(k == 0, breadth - 1, k - 1)
                here = (lane_q == k) | (lane_q == before)
                if f % 2 == 0:
                    even = jnp.where(here, turned, even)
                else:
                    odd = jnp.where(here, turned, odd)
                if q == 0:
                    send_v[0, pl.ds(f * levels + l, 1), :] = held[f, l, 0:1, :]
                if q == quarters - 1:
                    send_v[1, pl.ds(f * levels + l, 1), :] = held[f, l, height - 1 : height, :]
            su = su + x[0]
            sv = sv + x[1]
            sp = sp + weight * (haline * x[3] - thermal * x[2])
            return even, odd, su, sv, sp

        zero = jnp.zeros((QROWS, breadth), jnp.float32)
        even, odd, su, sv, sp = lax.fori_loop(0, levels, level_step, (zero,) * 5, unroll=2)
        mask = ext[0, PAD + r0 : PAD + r0 + QROWS, 0:breadth]
        head = jnp.where(even_q, even, odd) * mask[:, 0:1]
        tail = jnp.where(even_q, odd, even) * mask[:, breadth - 1 : breadth]
        send_w[0, r0 : r0 + QROWS, :] = head
        send_e[0, r0 : r0 + QROWS, :] = tail
        inv = 1.0 / levels
        ext[3, PAD + r0 : PAD + r0 + QROWS, 0:breadth] = su * inv * mask
        ext[4, PAD + r0 : PAD + r0 + QROWS, 0:breadth] = sv * inv * mask
        ext[5, PAD + r0 : PAD + r0 + QROWS, 0:breadth] = sp * mask

    packed = jnp.zeros((height, breadth), jnp.float32)
    for a in range(NA):
        x = ext[a, PAD : PAD + height, 0:breadth]
        packed = jnp.where(lane // STRIP == a, roll(x, STRIP * a + S8, 1), packed)
        n3 = NF * levels + S8 * a
        send_v[0, n3 : n3 + S8, :] = x[0:S8, :]
        send_v[1, n3 : n3 + S8, :] = x[height - S8 : height, :]
    send_e[1] = packed
    send_w[1] = packed
    for f in range(NF):
        send_v[0, f * levels : (f + 1) * levels, :] *= ocean[0:1, :]
        send_v[1, f * levels : (f + 1) * levels, :] *= ocean[height - 1 : height, :]

    count = (
        (n_lon - 1) + (n_lat - 1)
        + 2 * (lat > 0).astype(jnp.int32) + 2 * (lat < n_lat - 1).astype(jnp.int32)
    )
    pl.semaphore_wait(barrier, count)

    def remote(src, dst, number, recv_number, a, b):
        return pltpu.make_async_remote_copy(
            src_ref=src, dst_ref=dst,
            send_sem=send_sem.at[number], recv_sem=recv_sem.at[recv_number],
            device_id={"lon": a, "lat": b}, device_id_type=pl.DeviceIdType.MESH,
        )

    up_slot = jnp.where(last, 1, 0)
    up_lat = jnp.where(last, lat, lat + 1)
    up_lon = jnp.where(last, mirror, lon)
    up_e = jnp.where(last, lax.rem(mirror + 1, n_lon), west)
    up_w = jnp.where(last, lax.rem(mirror + n_lon - 1, n_lon), east)
    top = send_e.at[1, pl.ds(height - S8, S8), :]
    bottom = send_e.at[1, pl.ds(0, S8), :]
    go_up = remote(send_v.at[1], recv_v.at[up_slot], 2, 2 + up_slot, up_lon, up_lat)
    go_e = remote(send_e, recv_w, 0, 0, east, lat)
    go_w = remote(send_w, recv_e, 1, 1, west, lat)
    go_up_e = remote(top, recv_c.at[up_slot, 0], 4, 4 + 2 * up_slot, up_e, up_lat)
    go_up_w = remote(top, recv_c.at[up_slot, 1], 5, 5 + 2 * up_slot, up_w, up_lat)
    down_lat = jnp.where(lat > 0, lat - 1, lat + 1)
    go_down = remote(send_v.at[0], recv_v.at[1], 3, 3, lon, down_lat)
    go_down_e = remote(bottom, recv_c.at[1, 0], 6, 6, west, down_lat)
    go_down_w = remote(bottom, recv_c.at[1, 1], 7, 7, east, down_lat)
    self_e = last & (up_e == lon)
    self_w = last & (up_w == lon)
    go_up.start()
    go_e.start()
    go_w.start()

    @pl.when(lat > 0)
    def _():
        go_down.start()
        go_down_e.start()
        go_down_w.start()

    @pl.when(jnp.logical_not(self_e))
    def _():
        go_up_e.start()

    @pl.when(jnp.logical_not(self_w))
    def _():
        go_up_w.start()

    @pl.when(self_e)
    def _():
        recv_c[1, 0] = send_e[1, height - S8 : height, :]

    @pl.when(self_w)
    def _():
        recv_c[1, 1] = send_e[1, height - S8 : height, :]

    def arrive(dst, recv_number):
        remote(dst, dst, 0, recv_number, east, lat).wait_recv()

    arrive(recv_w, 0)
    arrive(recv_e, 1)
    arrive(recv_v.at[1], 3)

    @pl.when(jnp.logical_not(self_e))
    def _():
        arrive(recv_c.at[1, 0], 6)

    @pl.when(jnp.logical_not(self_w))
    def _():
        arrive(recv_c.at[1, 1], 7)

    @pl.when(lat > 0)
    def _():
        arrive(recv_v.at[0], 2)
        arrive(recv_c.at[0, 0], 4)
        arrive(recv_c.at[0, 1], 5)

    @pl.when(lat == 0)
    def _():
        recv_v[0] = jnp.zeros(recv_v.shape[1:], jnp.float32)
        recv_c[0] = jnp.zeros(recv_c.shape[1:], jnp.float32)

    even_lane = lax.rem(lane, 2) == 0
    edge_ref[0] = jnp.where(even_lane, recv_e[0], recv_w[0])
    edge_ref[1] = jnp.where(even_lane, recv_w[0], recv_e[0])
    for f in range(NF):
        rows_ref[0, f] = recv_v[0, f * levels : (f + 1) * levels, :]
        top_rows = recv_v[1, f * levels : (f + 1) * levels, :]
        turned = reverse_lanes(top_rows)
        rows_ref[1, f] = jnp.where(last, -turned if f < 2 else turned, top_rows)

    strip_e = lax.rem(lane, STRIP) >= S8
    halo_lane = (lane < S8) | (lane >= breadth - S8)
    side = jnp.where(strip_e, recv_e[1], recv_w[1])
    c_lane = lax.broadcasted_iota(jnp.int32, (S8, breadth), 1)
    c_strip_e = lax.rem(c_lane, STRIP) >= S8
    c_halo = (c_lane < S8) | (c_lane >= breadth - S8)
    corner = [jnp.where(c_strip_e, recv_c[j, 0], recv_c[j, 1]) for j in range(2)]
    end = PAD + height
    for a in range(NA):
        fill = 1.0 if a == 2 else 0.0
        shift = -(STRIP * a + S8)
        ext[a, PAD:end, breadth : 2 * breadth] = jnp.where(halo_lane, roll(side, shift, 1), fill)
        n3 = NF * levels + S8 * a
        s_mid = recv_v[0, n3 : n3 + S8, :]
        s_out = jnp.where(c_halo, roll(corner[0], shift, 1), fill)
        if a == 2:
            s_mid = jnp.where(lat == 0, 1.0, s_mid)
            s_out = jnp.where(lat == 0, 1.0, s_out)
        ext[a, 0:PAD, 0:breadth] = s_mid
        ext[a, 0:PAD, breadth : 2 * breadth] = s_out
        sign = -1.0 if a in (3, 4) else 1.0
        n_mid = recv_v[1, n3 : n3 + S8, :]
        n_out = jnp.where(c_halo, roll(corner[1], shift, 1), fill)
        for at, block in ((0, n_mid), (breadth, n_out)):
            turned = sign * reverse_lanes(block)
            turned = jnp.concatenate([turned[i : i + 1] for i in range(S8 - 1, -1, -1)], axis=0)
            ext[a, end : end + PAD, at : at + breadth] = jnp.where(last, turned, block)

    rows = lax.broadcasted_iota(jnp.int32, (height + 2 * PAD, 2 * breadth), 0) + (lat * height - PAD)
    total_rows = n_lat * height
    rows = jnp.where(rows >= total_rows, 2 * total_rows - 1 - rows, rows)
    coriolis = 2.0 * (rows.astype(jnp.float32) + 0.5) / total_rows - 1.0
    ocean_x, column, um, vm, pm = ext[0], ext[1], ext[3], ext[4], ext[5]
    nu, nv, np_ = near(um), near(vm), near(pm)
    u_mean = ocean_x * (
        um + time_step * (
            coriolis * vm - 0.5 * (np_[0] - np_[1])
            + viscosity * (nu[0] + nu[1] + nu[2] + nu[3] - 4.0 * um)
        )
    )
    v_mean = ocean_x * (
        vm + time_step * (
            -coriolis * um - 0.5 * (np_[2] - np_[3])
            + viscosity * (nv[0] + nv[1] + nv[2] + nv[3] - 4.0 * vm)
        )
    )
    is_open = column > 0.0
    nc = near(column)
    weights = [0.5 * (column + c) for c in nc]
    diag = ext[2] + weights[0] + weights[1] + weights[2] + weights[3]
    scale = jnp.where(is_open, 1.0 / diag, 0.0)
    rhs = (-0.5 * source_gain) * (
        roll(u_mean, -1, 1) - roll(u_mean, 1, 1) + roll(v_mean, -1, 0) - roll(v_mean, 1, 0)
    )
    basis = [scale * rhs]
    for _ in range(ITERS):
        ny = near(basis[-1])
        total = weights[0] * ny[0] + weights[1] * ny[1] + weights[2] * ny[2] + weights[3] * ny[3]
        basis.append(scale * total)
    inner = [y[PAD:end, 0:breadth] for y in basis]
    weight_in = diag[PAD:end, 0:breadth]
    weighted = [weight_in * y for y in inner]
    moments = []
    for m in range(2 * ITERS):
        moments.append(jnp.sum(inner[m // 2] * weighted[(m + 1) // 2], axis=0, keepdims=True))
    while len(moments) < 8:
        moments.append(jnp.zeros((1, breadth), jnp.float32))
    tile = jnp.concatenate(moments, axis=0)

    def gather_sum(tile, parts, me, n, sends, recvs, axis):
        parts[me] = tile
        copies = []
        for o in range(1, n):
            to = lax.rem(me + o, n)
            copy = pltpu.make_async_remote_copy(
                src_ref=parts.at[me], dst_ref=parts.at[me],
                send_sem=sends.at[o - 1], recv_sem=recvs.at[o - 1],
                device_id={axis: to}, device_id_type=pl.DeviceIdType.MESH,
            )
            copy.start()
            copies.append(copy)
        for o in range(1, n):
            source = lax.rem(me + n - o, n)
            pltpu.make_async_remote_copy(
                src_ref=parts.at[source], dst_ref=parts.at[source],
                send_sem=sends.at[o - 1], recv_sem=recvs.at[o - 1],
                device_id={axis: source}, device_id_type=pl.DeviceIdType.MESH,
            ).wait_recv()
        total = parts[0]
        for i in range(1, n):
            total = total + parts[i]
        return total, copies

    tile, lon_copies = gather_sum(tile, part_lon, lon, n_lon, lon_send, lon_recv, "lon")
    tile, lat_copies = gather_sum(tile, part_lat, lat, n_lat, lat_send, lat_recv, "lat")
    sums = jnp.broadcast_to(jnp.sum(tile, axis=1, keepdims=True), tile.shape)
    m = [sums[i : i + 1, :] for i in range(2 * ITERS)]

    def dot(a, b):
        total = 0.0
        for i, p in enumerate(a):
            for j, q in enumerate(b):
                total = total + (p * q) * m[i + j]
        return total

    one = jnp.ones((1, breadth), jnp.float32)
    z, d = [one], [one]
    x = []
    rz = m[0]
    for step in range(ITERS):
        image = [d[0]] + [d[i] - d[i - 1] for i in range(1, len(d))] + [-d[-1]]
        alpha = rz / dot(d, image)
        x = [alpha * d[i] + (x[i] if i < len(x) else 0.0) for i in range(len(d))]
        z = [(z[i] if i < len(z) else 0.0) - alpha * image[i] for i in range(len(image))]
        if step + 1 < ITERS:
            rz_new = dot(z, z)
            beta = rz_new / rz
            d = [z[i] + (beta * d[i] if i < len(d) else 0.0) for i in range(len(z))]
            rz = rz_new
    answer = x[0] * inner[0]
    for i in range(1, ITERS):
        answer = answer + x[i] * inner[i]
    left = z[0] * weighted[0]
    for i in range(1, ITERS + 1):
        left = left + z[i] * weighted[i]
    sol_ref[...] = answer
    res_ref[...] = left

    go_up.wait_send()
    go_e.wait_send()
    go_w.wait_send()

    @pl.when(lat > 0)
    def _():
        go_down.wait_send()
        go_down_e.wait_send()
        go_down_w.wait_send()

    @pl.when(jnp.logical_not(self_e))
    def _():
        go_up_e.wait_send()

    @pl.when(jnp.logical_not(self_w))
    def _():
        go_up_w.wait_send()

    for copy in lon_copies + lat_copies:
        copy.wait_send()


def update_kernel(
    u_ref, v_ref, t_ref, s_ref, marine_ref, edge_ref, rows_ref,
    u_out, v_out, t_out, s_out,
    held, done, padded, slope, load_sem, store_sem,
):
    lat = lax.axis_index("lat")
    levels, height, breadth = u_ref.shape
    fields, outs = (u_ref, v_ref, t_ref, s_ref), (u_out, v_out, t_out, s_out)
    chunk = 4 if levels % 4 == 0 else 1
    chunks = levels // chunk

    def load(c, f):
        part = pl.ds(c * chunk, chunk)
        return pltpu.make_async_copy(fields[f].at[part], held.at[f, part], load_sem.at[c, f])

    def store(c, f):
        part = pl.ds(c * chunk, chunk)
        return pltpu.make_async_copy(done.at[f, part], outs[f].at[part], store_sem.at[c, f])

    for c in range(chunks):
        for f in range(NF):
            load(c, f).start()
    slope[...] = jnp.zeros_like(slope)
    total_rows = lax.axis_size("lat") * height
    lane = lax.broadcasted_iota(jnp.int32, (8, breadth), 1)
    first_lane, last_lane = lane == 0, lane == breadth - 1
    row8 = lax.broadcasted_iota(jnp.int32, (8, breadth), 0)
    mul_q = (time_step * viscosity, time_step * viscosity, time_step * diffusivity, time_step * diffusivity)

    def level_step(l, carry):
        b = lax.rem(l, 2)
        for f in range(NF):
            padded[b, f, PAD - 1 : PAD, :] = rows_ref[0, f, pl.ds(l, 1), :]
            padded[b, f, PAD + height : PAD + height + 1, :] = rows_ref[1, f, pl.ds(l, 1), :]
            for g in range(height // 8):
                mask = marine_ref[8 * g : 8 * g + 8, :].astype(jnp.float32)
                padded[b, f, PAD + 8 * g : PAD + 8 * g + 8, :] = held[f, l, 8 * g : 8 * g + 8, :] * mask
        for g in range(height // 8):
            r = 8 * g
            mask = marine_ref[r : r + 8, :].astype(jnp.float32)
            coriolis = (
                2.0 * ((row8 + (lat * height + r)).astype(jnp.float32) + 0.5) / total_rows - 1.0
            ) * time_step
            x, e, w, n, s = [], [], [], [], []
            for f in range(NF):
                at = PAD + r
                here = padded[b, f, at : at + 8, :]
                k = NF * l + f
                halo = pltpu.roll(
                    edge_ref[f % 2, r : r + 8, :], jnp.where(k == 0, 0, breadth - k), 1
                )
                x.append(here)
                e.append(pltpu.roll(jnp.where(first_lane, halo, here), breadth - 1, 1))
                w.append(pltpu.roll(jnp.where(last_lane, halo, here), 1, 1))
                n.append(padded[b, f, at + 1 : at + 9, :])
                s.append(padded[b, f, at - 1 : at + 7, :])
            gx = slope[0, r : r + 8, :] + (haline * (e[3] - w[3]) - thermal * (e[2] - w[2]))
            gy = slope[1, r : r + 8, :] + (haline * (n[3] - s[3]) - thermal * (n[2] - s[2]))
            slope[0, r : r + 8, :] = gx
            slope[1, r : r + 8, :] = gy
            new = [
                x[f] + mul_q[f] * (e[f] + w[f] + n[f] + s[f] - 4.0 * x[f]) for f in range(NF)
            ]
            new[0] = new[0] + (coriolis * x[1] - (0.5 * time_step) * gx)
            new[1] = new[1] - (coriolis * x[0] + (0.5 * time_step) * gy)
            for f in (2, 3):
                flux = e[0] * e[f] - w[0] * w[f] + n[1] * n[f] - s[1] * s[f]
                new[f] = new[f] - (0.5 * time_step) * flux
            for f in range(NF):
                done[f, l, r : r + 8, :] = mask * new[f]
        return carry

    for c in range(chunks):
        for f in range(NF):
            load(c, f).wait()
        lax.fori_loop(c * chunk, (c + 1) * chunk, level_step, 0)
        for f in range(NF):
            store(c, f).start()
    for c in range(chunks):
        for f in range(NF):
            store(c, f).wait()


def local(
    zonal_current, meridional_current, warmth_anomaly, brine_anomaly,
    marine_indicator, retained_tile_indicator, seabed_thickness, elevation_pivot_entry,
):
    levels, height, breadth = zonal_current.shape
    n_lon, n_lat = lax.axis_size("lon"), lax.axis_size("lat")
    f32 = jnp.float32
    any_spec = pl.BlockSpec(memory_space=pl.ANY)
    vmem = pl.BlockSpec(memory_space=pltpu.VMEM)
    smem = pl.BlockSpec(memory_space=pltpu.SMEM)
    chunk = 4 if levels % 4 == 0 else 1
    quarters = height // QROWS
    wide = NF * levels + NA * S8
    dma = pltpu.SemaphoreType.DMA
    fields = (zonal_current, meridional_current, warmth_anomaly, brine_anomaly)
    edge, rows, answer, left = pl.pallas_call(
        surface_kernel,
        out_shape=(
            jax.ShapeDtypeStruct((2, height, breadth), f32),
            jax.ShapeDtypeStruct((2, NF, levels, breadth), f32),
            jax.ShapeDtypeStruct((height, breadth), f32),
            jax.ShapeDtypeStruct((height, breadth), f32),
        ),
        in_specs=[any_spec] * 4 + [vmem, smem, vmem, vmem],
        out_specs=(vmem,) * 4,
        scratch_shapes=[
            pltpu.VMEM((NF, levels, height, breadth), f32),
            pltpu.VMEM((2, height, breadth), f32),
            pltpu.VMEM((2, height, breadth), f32),
            pltpu.VMEM((2, wide, breadth), f32),
            pltpu.VMEM((2, height, breadth), f32),
            pltpu.VMEM((2, height, breadth), f32),
            pltpu.VMEM((2, wide, breadth), f32),
            pltpu.VMEM((2, 2, S8, breadth), f32),
            pltpu.VMEM((NA, height + 2 * PAD, 2 * breadth), f32),
            pltpu.VMEM((n_lon, 8, breadth), f32),
            pltpu.VMEM((n_lat, 8, breadth), f32),
            dma((quarters, NF)),
            dma((8,)),
            dma((8,)),
            dma((n_lon - 1,)),
            dma((n_lon - 1,)),
            dma((n_lat - 1,)),
            dma((n_lat - 1,)),
        ],
        compiler_params=pltpu.CompilerParams(
            collective_id=0, has_side_effects=True, vmem_limit_bytes=24 * 2**20
        ),
        name="surface",
    )(*fields, marine_indicator, retained_tile_indicator, seabed_thickness, elevation_pivot_entry)
    new = pl.pallas_call(
        update_kernel,
        out_shape=tuple(jax.ShapeDtypeStruct(x.shape, f32) for x in fields),
        in_specs=[any_spec] * 4 + [vmem] * 3,
        out_specs=(any_spec,) * 4,
        scratch_shapes=[
            pltpu.VMEM((NF, levels, height, breadth), f32),
            pltpu.VMEM((NF, levels, height, breadth), f32),
            pltpu.VMEM((2, NF, height + 2 * PAD, breadth), f32),
            pltpu.VMEM((2, height, breadth), f32),
            dma((levels // chunk, NF)),
            dma((levels // chunk, NF)),
        ],
        compiler_params=pltpu.CompilerParams(vmem_limit_bytes=24 * 2**20),
        name="update",
    )(*fields, marine_indicator, edge, rows)
    return (*new, answer, left)


def solution(mesh):
    cube, flat = P(None, "lat", "lon"), P("lat", "lon")
    return jax.shard_map(
        local,
        mesh=mesh,
        in_specs=(cube,) * 4 + (flat,) * 4,
        out_specs=(cube,) * 4 + (flat,) * 2,
        check_vma=False,
    )
```

```python
import functools

import jax
import jax.numpy as jnp
from jax import lax
from jax.experimental import pallas as pl
from jax.experimental.pallas import tpu as pltpu
from jax.sharding import PartitionSpec as P

BLK = 16
ITERS = 3

time_step = 0.1
viscosity = 0.2
diffusivity = 0.15
thermal = 0.2
haline = 0.8
source_gain = 8.0

NF = 4
NA = 6
STRIP = 16
S8 = 8
QROWS = 32
PAD = 8


def reverse_lanes(x):
    index = x.shape[-1] - 1 - lax.broadcasted_iota(jnp.int32, x.shape, x.ndim - 1)
    return jnp.take_along_axis(x, index, axis=x.ndim - 1, mode="promise_in_bounds")


def roll(x, shift, axis):
    return pltpu.roll(x, shift % x.shape[axis], axis)


def near(x):
    return roll(x, -1, 1), roll(x, 1, 1), roll(x, -1, 0), roll(x, 1, 0)


def surface_kernel(
    u_ref, v_ref, t_ref, s_ref, marine_hbm, kept_hbm, depth_hbm, elev_hbm,
    edge_ref, rows_ref, sol_ref, res_ref,
    held, send_e, send_w, send_v, recv_e, recv_w, recv_v, recv_c, ext,
    part_lon, part_lat, marine_ref, kept_ref, depth_ref, elev_ref, flat_sem, load_sem, send_sem, recv_sem, lon_send, lon_recv, lat_send, lat_recv,
):
    n_lon, n_lat = lax.axis_size("lon"), lax.axis_size("lat")
    lon, lat = lax.axis_index("lon"), lax.axis_index("lat")
    levels, height, breadth = u_ref.shape
    last = lat == n_lat - 1
    east, west = lax.rem(lon + 1, n_lon), lax.rem(lon + n_lon - 1, n_lon)
    mirror = n_lon - 1 - lon

    flat = [
        pltpu.make_async_copy(src, dst, flat_sem.at[i])
        for i, (src, dst) in enumerate(
            ((marine_hbm, marine_ref), (kept_hbm, kept_ref), (depth_hbm, depth_ref), (elev_hbm, elev_ref))
        )
    ]
    for copy in flat:
        copy.start()
    fields = (u_ref, v_ref, t_ref, s_ref)
    quarters = height // QROWS
    loads = []
    for q in range(quarters):
        row = []
        for f in range(NF):
            copy = pltpu.make_async_copy(
                fields[f].at[:, pl.ds(q * QROWS, QROWS), :],
                held.at[f, :, pl.ds(q * QROWS, QROWS), :],
                load_sem.at[q, f],
            )
            copy.start()
            row.append(copy)
        loads.append(row)

    barrier = pltpu.get_barrier_semaphore()

    def greet(a, b):
        pl.semaphore_signal(
            barrier, inc=1, device_id={"lon": a, "lat": b}, device_id_type=pl.DeviceIdType.MESH
        )

    for o in range(1, n_lon):
        greet(lax.rem(lon + o, n_lon), lat)
    for o in range(1, n_lat):
        greet(lon, lax.rem(lat + o, n_lat))

    @pl.when(lat > 0)
    def _():
        greet(east, lat - 1)
        greet(west, lat - 1)

    @pl.when(lat < n_lat - 1)
    def _():
        greet(east, lat + 1)
        greet(west, lat + 1)

    for copy in flat:
        copy.wait()
    lane = lax.broadcasted_iota(jnp.int32, (height, breadth), 1)
    ocean = marine_ref[...].astype(jnp.float32)
    bands = []
    lane_band = lax.broadcasted_iota(jnp.int32, (BLK, breadth), 1) // BLK
    for jb in range(height // BLK):
        band = jnp.zeros((BLK, breadth), jnp.float32)
        for ib in range(breadth // BLK):
            band = jnp.where(lane_band == ib, kept_ref[jb, ib].astype(jnp.float32), band)
        bands.append(band)
    kept = jnp.concatenate(bands, axis=0)
    ext[0, PAD : PAD + height, 0:breadth] = ocean
    ext[1, PAD : PAD + height, 0:breadth] = depth_ref[...] * (ocean * kept)
    ext[2, PAD : PAD + height, 0:breadth] = elev_ref[...]

    lane_q = lax.broadcasted_iota(jnp.int32, (QROWS, breadth), 1)
    even_q = lax.rem(lane_q, 2) == 0
    for q in range(quarters):
        for copy in loads[q]:
            copy.wait()
        r0 = q * QROWS

        def level_step(l, carry, r0=r0, q=q):
            even, odd, su, sv, sp = carry
            weight = (levels - l).astype(jnp.float32) * (1.0 / levels)
            x = [held[f, l, r0 : r0 + QROWS, :] for f in range(NF)]
            for f in range(NF):
                k = NF * l + f
                turned = pltpu.roll(x[f], k, 1)
                before = jnp.where(k == 0, breadth - 1, k - 1)
                here = (lane_q == k) | (lane_q == before)
                if f % 2 == 0:
                    even = jnp.where(here, turned, even)
                else:
                    odd = jnp.where(here, turned, odd)
                if q == 0:
                    send_v[0, pl.ds(f * levels + l, 1), :] = held[f, l, 0:1, :]
                if q == quarters - 1:
                    send_v[1, pl.ds(f * levels + l, 1), :] = held[f, l, height - 1 : height, :]
            su = su + x[0]
            sv = sv + x[1]
            sp = sp + weight * (haline * x[3] - thermal * x[2])
            return even, odd, su, sv, sp

        zero = jnp.zeros((QROWS, breadth), jnp.float32)
        even, odd, su, sv, sp = lax.fori_loop(0, levels, level_step, (zero,) * 5, unroll=2)
        mask = ext[0, PAD + r0 : PAD + r0 + QROWS, 0:breadth]
        head = jnp.where(even_q, even, odd) * mask[:, 0:1]
        tail = jnp.where(even_q, odd, even) * mask[:, breadth - 1 : breadth]
        send_w[0, r0 : r0 + QROWS, :] = head
        send_e[0, r0 : r0 + QROWS, :] = tail
        inv = 1.0 / levels
        ext[3, PAD + r0 : PAD + r0 + QROWS, 0:breadth] = su * inv * mask
        ext[4, PAD + r0 : PAD + r0 + QROWS, 0:breadth] = sv * inv * mask
        ext[5, PAD + r0 : PAD + r0 + QROWS, 0:breadth] = sp * mask

    packed = jnp.zeros((height, breadth), jnp.float32)
    for a in range(NA):
        x = ext[a, PAD : PAD + height, 0:breadth]
        packed = jnp.where(lane // STRIP == a, roll(x, STRIP * a + S8, 1), packed)
        n3 = NF * levels + S8 * a
        send_v[0, n3 : n3 + S8, :] = x[0:S8, :]
        send_v[1, n3 : n3 + S8, :] = x[height - S8 : height, :]
    send_e[1] = packed
    send_w[1] = packed
    for f in range(NF):
        send_v[0, f * levels : (f + 1) * levels, :] *= ocean[0:1, :]
        send_v[1, f * levels : (f + 1) * levels, :] *= ocean[height - 1 : height, :]

    count = (
        (n_lon - 1) + (n_lat - 1)
        + 2 * (lat > 0).astype(jnp.int32) + 2 * (lat < n_lat - 1).astype(jnp.int32)
    )
    pl.semaphore_wait(barrier, count)

    def remote(src, dst, number, recv_number, a, b):
        return pltpu.make_async_remote_copy(
            src_ref=src, dst_ref=dst,
            send_sem=send_sem.at[number], recv_sem=recv_sem.at[recv_number],
            device_id={"lon": a, "lat": b}, device_id_type=pl.DeviceIdType.MESH,
        )

    up_slot = jnp.where(last, 1, 0)
    up_lat = jnp.where(last, lat, lat + 1)
    up_lon = jnp.where(last, mirror, lon)
    up_e = jnp.where(last, lax.rem(mirror + 1, n_lon), west)
    up_w = jnp.where(last, lax.rem(mirror + n_lon - 1, n_lon), east)
    top = send_e.at[1, pl.ds(height - S8, S8), :]
    bottom = send_e.at[1, pl.ds(0, S8), :]
    go_up = remote(send_v.at[1], recv_v.at[up_slot], 2, 2 + up_slot, up_lon, up_lat)
    go_e = remote(send_e, recv_w, 0, 0, east, lat)
    go_w = remote(send_w, recv_e, 1, 1, west, lat)
    go_up_e = remote(top, recv_c.at[up_slot, 0], 4, 4 + 2 * up_slot, up_e, up_lat)
    go_up_w = remote(top, recv_c.at[up_slot, 1], 5, 5 + 2 * up_slot, up_w, up_lat)
    down_lat = jnp.where(lat > 0, lat - 1, lat + 1)
    go_down = remote(send_v.at[0], recv_v.at[1], 3, 3, lon, down_lat)
    go_down_e = remote(bottom, recv_c.at[1, 0], 6, 6, west, down_lat)
    go_down_w = remote(bottom, recv_c.at[1, 1], 7, 7, east, down_lat)
    self_e = last & (up_e == lon)
    self_w = last & (up_w == lon)
    go_up.start()
    go_e.start()
    go_w.start()

    @pl.when(lat > 0)
    def _():
        go_down.start()
        go_down_e.start()
        go_down_w.start()

    @pl.when(jnp.logical_not(self_e))
    def _():
        go_up_e.start()

    @pl.when(jnp.logical_not(self_w))
    def _():
        go_up_w.start()

    @pl.when(self_e)
    def _():
        recv_c[1, 0] = send_e[1, height - S8 : height, :]

    @pl.when(self_w)
    def _():
        recv_c[1, 1] = send_e[1, height - S8 : height, :]

    def arrive(dst, recv_number):
        remote(dst, dst, 0, recv_number, east, lat).wait_recv()

    arrive(recv_w, 0)
    arrive(recv_e, 1)
    arrive(recv_v.at[1], 3)

    @pl.when(jnp.logical_not(self_e))
    def _():
        arrive(recv_c.at[1, 0], 6)

    @pl.when(jnp.logical_not(self_w))
    def _():
        arrive(recv_c.at[1, 1], 7)

    @pl.when(lat > 0)
    def _():
        arrive(recv_v.at[0], 2)
        arrive(recv_c.at[0, 0], 4)
        arrive(recv_c.at[0, 1], 5)

    @pl.when(lat == 0)
    def _():
        recv_v[0] = jnp.zeros(recv_v.shape[1:], jnp.float32)
        recv_c[0] = jnp.zeros(recv_c.shape[1:], jnp.float32)

    even_lane = lax.rem(lane, 2) == 0
    edge_ref[0] = jnp.where(even_lane, recv_e[0], recv_w[0])
    edge_ref[1] = jnp.where(even_lane, recv_w[0], recv_e[0])
    for f in range(NF):
        rows_ref[0, f] = recv_v[0, f * levels : (f + 1) * levels, :]
        top_rows = recv_v[1, f * levels : (f + 1) * levels, :]
        turned = reverse_lanes(top_rows)
        rows_ref[1, f] = jnp.where(last, -turned if f < 2 else turned, top_rows)

    strip_e = lax.rem(lane, STRIP) >= S8
    halo_lane = (lane < S8) | (lane >= breadth - S8)
    side = jnp.where(strip_e, recv_e[1], recv_w[1])
    c_lane = lax.broadcasted_iota(jnp.int32, (S8, breadth), 1)
    c_strip_e = lax.rem(c_lane, STRIP) >= S8
    c_halo = (c_lane < S8) | (c_lane >= breadth - S8)
    corner = [jnp.where(c_strip_e, recv_c[j, 0], recv_c[j, 1]) for j in range(2)]
    end = PAD + height
    for a in range(NA):
        fill = 1.0 if a == 2 else 0.0
        shift = -(STRIP * a + S8)
        ext[a, PAD:end, breadth : 2 * breadth] = jnp.where(halo_lane, roll(side, shift, 1), fill)
        n3 = NF * levels + S8 * a
        s_mid = recv_v[0, n3 : n3 + S8, :]
        s_out = jnp.where(c_halo, roll(corner[0], shift, 1), fill)
        if a == 2:
            s_mid = jnp.where(lat == 0, 1.0, s_mid)
            s_out = jnp.where(lat == 0, 1.0, s_out)
        ext[a, 0:PAD, 0:breadth] = s_mid
        ext[a, 0:PAD, breadth : 2 * breadth] = s_out
        sign = -1.0 if a in (3, 4) else 1.0
        n_mid = recv_v[1, n3 : n3 + S8, :]
        n_out = jnp.where(c_halo, roll(corner[1], shift, 1), fill)
        for at, block in ((0, n_mid), (breadth, n_out)):
            turned = sign * reverse_lanes(block)
            turned = jnp.concatenate([turned[i : i + 1] for i in range(S8 - 1, -1, -1)], axis=0)
            ext[a, end : end + PAD, at : at + breadth] = jnp.where(last, turned, block)

    rows = lax.broadcasted_iota(jnp.int32, (height + 2 * PAD, 2 * breadth), 0) + (lat * height - PAD)
    total_rows = n_lat * height
    rows = jnp.where(rows >= total_rows, 2 * total_rows - 1 - rows, rows)
    coriolis = 2.0 * (rows.astype(jnp.float32) + 0.5) / total_rows - 1.0
    ocean_x, column, um, vm, pm = ext[0], ext[1], ext[3], ext[4], ext[5]
    nu, nv, np_ = near(um), near(vm), near(pm)
    u_mean = ocean_x * (
        um + time_step * (
            coriolis * vm - 0.5 * (np_[0] - np_[1])
            + viscosity * (nu[0] + nu[1] + nu[2] + nu[3] - 4.0 * um)
        )
    )
    v_mean = ocean_x * (
        vm + time_step * (
            -coriolis * um - 0.5 * (np_[2] - np_[3])
            + viscosity * (nv[0] + nv[1] + nv[2] + nv[3] - 4.0 * vm)
        )
    )
    is_open = column > 0.0
    nc = near(column)
    weights = [0.5 * (column + c) for c in nc]
    diag = ext[2] + weights[0] + weights[1] + weights[2] + weights[3]
    scale = jnp.where(is_open, 1.0 / diag, 0.0)
    rhs = (-0.5 * source_gain) * (
        roll(u_mean, -1, 1) - roll(u_mean, 1, 1) + roll(v_mean, -1, 0) - roll(v_mean, 1, 0)
    )
    basis = [scale * rhs]
    for _ in range(ITERS):
        ny = near(basis[-1])
        total = weights[0] * ny[0] + weights[1] * ny[1] + weights[2] * ny[2] + weights[3] * ny[3]
        basis.append(scale * total)
    inner = [y[PAD:end, 0:breadth] for y in basis]
    weight_in = diag[PAD:end, 0:breadth]
    weighted = [weight_in * y for y in inner]
    moments = []
    for m in range(2 * ITERS):
        moments.append(jnp.sum(inner[m // 2] * weighted[(m + 1) // 2], axis=0, keepdims=True))
    while len(moments) < 8:
        moments.append(jnp.zeros((1, breadth), jnp.float32))
    tile = jnp.concatenate(moments, axis=0)

    def gather_sum(tile, parts, me, n, sends, recvs, axis):
        parts[me] = tile
        copies = []
        for o in range(1, n):
            to = lax.rem(me + o, n)
            copy = pltpu.make_async_remote_copy(
                src_ref=parts.at[me], dst_ref=parts.at[me],
                send_sem=sends.at[o - 1], recv_sem=recvs.at[o - 1],
                device_id={axis: to}, device_id_type=pl.DeviceIdType.MESH,
            )
            copy.start()
            copies.append(copy)
        for o in range(1, n):
            source = lax.rem(me + n - o, n)
            pltpu.make_async_remote_copy(
                src_ref=parts.at[source], dst_ref=parts.at[source],
                send_sem=sends.at[o - 1], recv_sem=recvs.at[o - 1],
                device_id={axis: source}, device_id_type=pl.DeviceIdType.MESH,
            ).wait_recv()
        total = parts[0]
        for i in range(1, n):
            total = total + parts[i]
        return total, copies

    tile, lon_copies = gather_sum(tile, part_lon, lon, n_lon, lon_send, lon_recv, "lon")
    tile, lat_copies = gather_sum(tile, part_lat, lat, n_lat, lat_send, lat_recv, "lat")
    sums = jnp.broadcast_to(jnp.sum(tile, axis=1, keepdims=True), tile.shape)
    m = [sums[i : i + 1, :] for i in range(2 * ITERS)]

    def dot(a, b):
        total = 0.0
        for i, p in enumerate(a):
            for j, q in enumerate(b):
                total = total + (p * q) * m[i + j]
        return total

    one = jnp.ones((1, breadth), jnp.float32)
    z, d = [one], [one]
    x = []
    rz = m[0]
    for step in range(ITERS):
        image = [d[0]] + [d[i] - d[i - 1] for i in range(1, len(d))] + [-d[-1]]
        alpha = rz / dot(d, image)
        x = [alpha * d[i] + (x[i] if i < len(x) else 0.0) for i in range(len(d))]
        z = [(z[i] if i < len(z) else 0.0) - alpha * image[i] for i in range(len(image))]
        if step + 1 < ITERS:
            rz_new = dot(z, z)
            beta = rz_new / rz
            d = [z[i] + (beta * d[i] if i < len(d) else 0.0) for i in range(len(z))]
            rz = rz_new
    answer = x[0] * inner[0]
    for i in range(1, ITERS):
        answer = answer + x[i] * inner[i]
    left = z[0] * weighted[0]
    for i in range(1, ITERS + 1):
        left = left + z[i] * weighted[i]
    sol_ref[...] = answer
    res_ref[...] = left

    go_up.wait_send()
    go_e.wait_send()
    go_w.wait_send()

    @pl.when(lat > 0)
    def _():
        go_down.wait_send()
        go_down_e.wait_send()
        go_down_w.wait_send()

    @pl.when(jnp.logical_not(self_e))
    def _():
        go_up_e.wait_send()

    @pl.when(jnp.logical_not(self_w))
    def _():
        go_up_w.wait_send()

    for copy in lon_copies + lat_copies:
        copy.wait_send()


def update_kernel(
    u_ref, v_ref, t_ref, s_ref, marine_hbm, edge_ref, rows_ref, answer_ref, left_ref,
    u_out, v_out, t_out, s_out, answer_out, left_out,
    held, done, padded, slope, marine_ref, load_sem, store_sem, flat_sem,
):
    lat = lax.axis_index("lat")
    levels, height, breadth = u_ref.shape
    fields, outs = (u_ref, v_ref, t_ref, s_ref), (u_out, v_out, t_out, s_out)
    chunk = 4 if levels % 4 == 0 else 1
    chunks = levels // chunk

    def load(c, f):
        part = pl.ds(c * chunk, chunk)
        return pltpu.make_async_copy(fields[f].at[part], held.at[f, part], load_sem.at[c, f])

    def store(c, f):
        part = pl.ds(c * chunk, chunk)
        return pltpu.make_async_copy(done.at[f, part], outs[f].at[part], store_sem.at[c, f])

    flat = [
        pltpu.make_async_copy(src, dst, flat_sem.at[i])
        for i, (src, dst) in enumerate(
            ((marine_hbm, marine_ref), (answer_ref, answer_out), (left_ref, left_out))
        )
    ]
    flat[0].start()
    for c in range(chunks):
        for f in range(NF):
            load(c, f).start()
    flat[1].start()
    flat[2].start()
    slope[...] = jnp.zeros_like(slope)
    total_rows = lax.axis_size("lat") * height
    lane = lax.broadcasted_iota(jnp.int32, (8, breadth), 1)
    first_lane, last_lane = lane == 0, lane == breadth - 1
    row8 = lax.broadcasted_iota(jnp.int32, (8, breadth), 0)
    mul_q = (time_step * viscosity, time_step * viscosity, time_step * diffusivity, time_step * diffusivity)

    flat[0].wait()

    def level_step(l, carry):
        b = lax.rem(l, 2)
        for f in range(NF):
            padded[b, f, PAD - 1 : PAD, :] = rows_ref[0, f, pl.ds(l, 1), :]
            padded[b, f, PAD + height : PAD + height + 1, :] = rows_ref[1, f, pl.ds(l, 1), :]
            for g in range(height // 8):
                mask = marine_ref[8 * g : 8 * g + 8, :].astype(jnp.float32)
                padded[b, f, PAD + 8 * g : PAD + 8 * g + 8, :] = held[f, l, 8 * g : 8 * g + 8, :] * mask
        for g in range(height // 8):
            r = 8 * g
            mask = marine_ref[r : r + 8, :].astype(jnp.float32)
            coriolis = (
                2.0 * ((row8 + (lat * height + r)).astype(jnp.float32) + 0.5) / total_rows - 1.0
            ) * time_step
            x, e, w, n, s = [], [], [], [], []
            for f in range(NF):
                at = PAD + r
                here = padded[b, f, at : at + 8, :]
                k = NF * l + f
                halo = pltpu.roll(
                    edge_ref[f % 2, r : r + 8, :], jnp.where(k == 0, 0, breadth - k), 1
                )
                x.append(here)
                e.append(pltpu.roll(jnp.where(first_lane, halo, here), breadth - 1, 1))
                w.append(pltpu.roll(jnp.where(last_lane, halo, here), 1, 1))
                n.append(padded[b, f, at + 1 : at + 9, :])
                s.append(padded[b, f, at - 1 : at + 7, :])
            gx = slope[0, r : r + 8, :] + (haline * (e[3] - w[3]) - thermal * (e[2] - w[2]))
            gy = slope[1, r : r + 8, :] + (haline * (n[3] - s[3]) - thermal * (n[2] - s[2]))
            slope[0, r : r + 8, :] = gx
            slope[1, r : r + 8, :] = gy
            new = [
                x[f] + mul_q[f] * (e[f] + w[f] + n[f] + s[f] - 4.0 * x[f]) for f in range(NF)
            ]
            new[0] = new[0] + (coriolis * x[1] - (0.5 * time_step) * gx)
            new[1] = new[1] - (coriolis * x[0] + (0.5 * time_step) * gy)
            for f in (2, 3):
                flux = e[0] * e[f] - w[0] * w[f] + n[1] * n[f] - s[1] * s[f]
                new[f] = new[f] - (0.5 * time_step) * flux
            for f in range(NF):
                done[f, l, r : r + 8, :] = mask * new[f]
        return carry

    for c in range(chunks):
        for f in range(NF):
            load(c, f).wait()
        lax.fori_loop(c * chunk, (c + 1) * chunk, level_step, 0)
        for f in range(NF):
            store(c, f).start()
    for c in range(chunks):
        for f in range(NF):
            store(c, f).wait()
    flat[1].wait()
    flat[2].wait()


def local(
    zonal_current, meridional_current, warmth_anomaly, brine_anomaly,
    marine_indicator, retained_tile_indicator, seabed_thickness, elevation_pivot_entry,
):
    levels, height, breadth = zonal_current.shape
    n_lon, n_lat = lax.axis_size("lon"), lax.axis_size("lat")
    f32 = jnp.float32
    vmem = pl.BlockSpec(memory_space=pltpu.VMEM)
    hbm = pl.BlockSpec(memory_space=pltpu.HBM)
    chunk = 4 if levels % 4 == 0 else 1
    quarters = height // QROWS
    wide = NF * levels + NA * S8
    dma = pltpu.SemaphoreType.DMA
    fields = (zonal_current, meridional_current, warmth_anomaly, brine_anomaly)
    edge, rows, answer, left = pl.pallas_call(
        surface_kernel,
        out_shape=(
            jax.ShapeDtypeStruct((2, height, breadth), f32),
            jax.ShapeDtypeStruct((2, NF, levels, breadth), f32),
            jax.ShapeDtypeStruct((height, breadth), f32),
            jax.ShapeDtypeStruct((height, breadth), f32),
        ),
        in_specs=[hbm] * 8,
        out_specs=(vmem,) * 4,
        scratch_shapes=[
            pltpu.VMEM((NF, levels, height, breadth), f32),
            pltpu.VMEM((2, height, breadth), f32),
            pltpu.VMEM((2, height, breadth), f32),
            pltpu.VMEM((2, wide, breadth), f32),
            pltpu.VMEM((2, height, breadth), f32),
            pltpu.VMEM((2, height, breadth), f32),
            pltpu.VMEM((2, wide, breadth), f32),
            pltpu.VMEM((2, 2, S8, breadth), f32),
            pltpu.VMEM((NA, height + 2 * PAD, 2 * breadth), f32),
            pltpu.VMEM((n_lon, 8, breadth), f32),
            pltpu.VMEM((n_lat, 8, breadth), f32),
            pltpu.VMEM((height, breadth), jnp.int32),
            pltpu.SMEM(retained_tile_indicator.shape, jnp.int32),
            pltpu.VMEM((height, breadth), f32),
            pltpu.VMEM((height, breadth), f32),
            dma((4,)),
            dma((quarters, NF)),
            dma((8,)),
            dma((8,)),
            dma((n_lon - 1,)),
            dma((n_lon - 1,)),
            dma((n_lat - 1,)),
            dma((n_lat - 1,)),
        ],
        compiler_params=pltpu.CompilerParams(
            collective_id=0, has_side_effects=True, vmem_limit_bytes=60 * 2**20
        ),
        name="surface",
    )(*fields, marine_indicator, retained_tile_indicator, seabed_thickness, elevation_pivot_entry)
    new = pl.pallas_call(
        update_kernel,
        out_shape=tuple(jax.ShapeDtypeStruct(x.shape, f32) for x in (*fields, answer, left)),
        in_specs=[hbm] * 5 + [vmem] * 2 + [hbm] * 2,
        out_specs=(hbm,) * 6,
        scratch_shapes=[
            pltpu.VMEM((NF, levels, height, breadth), f32),
            pltpu.VMEM((NF, levels, height, breadth), f32),
            pltpu.VMEM((2, NF, height + 2 * PAD, breadth), f32),
            pltpu.VMEM((2, height, breadth), f32),
            pltpu.VMEM((height, breadth), jnp.int32),
            dma((levels // chunk, NF)),
            dma((levels // chunk, NF)),
            dma((3,)),
        ],
        compiler_params=pltpu.CompilerParams(vmem_limit_bytes=60 * 2**20),
        name="update",
    )(*fields, marine_indicator, edge, rows, answer, left)
    return new


def solution(mesh):
    cube, flat = P(None, "lat", "lon"), P("lat", "lon")
    return jax.shard_map(
        local,
        mesh=mesh,
        in_specs=(cube,) * 4 + (flat,) * 4,
        out_specs=(cube,) * 4 + (flat,) * 2,
        check_vma=False,
    )
```

```python
import functools

import jax
import jax.numpy as jnp
from jax import lax
from jax.experimental import pallas as pl
from jax.experimental.pallas import tpu as pltpu
from jax.sharding import PartitionSpec as P

BLK = 16
ITERS = 3

time_step = 0.1
viscosity = 0.2
diffusivity = 0.15
thermal = 0.2
haline = 0.8
source_gain = 8.0

NF = 4
NA = 6
STRIP = 16
S8 = 8
QROWS = 32
PAD = 8


def reverse_lanes(x):
    index = x.shape[-1] - 1 - lax.broadcasted_iota(jnp.int32, x.shape, x.ndim - 1)
    return jnp.take_along_axis(x, index, axis=x.ndim - 1, mode="promise_in_bounds")


def roll(x, shift, axis):
    return pltpu.roll(x, shift % x.shape[axis], axis)


def near(x):
    return roll(x, -1, 1), roll(x, 1, 1), roll(x, -1, 0), roll(x, 1, 0)


def surface_kernel(
    u_ref, v_ref, t_ref, s_ref, marine_hbm, kept_hbm, depth_hbm, elev_hbm,
    u_mid, v_mid, t_mid, s_mid_, sol_ref, res_ref,
    edge_ref, rows_ref, done, padded, slope, store_sem, held, send_e, send_w, send_v, recv_e, recv_w, recv_v, recv_c, ext,
    part_lon, part_lat, marine_ref, kept_ref, depth_ref, elev_ref, flat_sem, load_sem, send_sem, recv_sem, lon_send, lon_recv, lat_send, lat_recv,
):
    n_lon, n_lat = lax.axis_size("lon"), lax.axis_size("lat")
    lon, lat = lax.axis_index("lon"), lax.axis_index("lat")
    levels, height, breadth = u_ref.shape
    last = lat == n_lat - 1
    east, west = lax.rem(lon + 1, n_lon), lax.rem(lon + n_lon - 1, n_lon)
    mirror = n_lon - 1 - lon

    flat = [
        pltpu.make_async_copy(src, dst, flat_sem.at[i])
        for i, (src, dst) in enumerate(
            ((marine_hbm, marine_ref), (kept_hbm, kept_ref), (depth_hbm, depth_ref), (elev_hbm, elev_ref))
        )
    ]
    for copy in flat:
        copy.start()
    fields = (u_ref, v_ref, t_ref, s_ref)
    quarters = height // QROWS
    loads = []
    for q in range(quarters):
        row = []
        for f in range(NF):
            copy = pltpu.make_async_copy(
                fields[f].at[:, pl.ds(q * QROWS, QROWS), :],
                held.at[f, :, pl.ds(q * QROWS, QROWS), :],
                load_sem.at[q, f],
            )
            copy.start()
            row.append(copy)
        loads.append(row)

    barrier = pltpu.get_barrier_semaphore()

    def greet(a, b):
        pl.semaphore_signal(
            barrier, inc=1, device_id={"lon": a, "lat": b}, device_id_type=pl.DeviceIdType.MESH
        )

    for o in range(1, n_lon):
        greet(lax.rem(lon + o, n_lon), lat)
    for o in range(1, n_lat):
        greet(lon, lax.rem(lat + o, n_lat))

    @pl.when(lat > 0)
    def _():
        greet(east, lat - 1)
        greet(west, lat - 1)

    @pl.when(lat < n_lat - 1)
    def _():
        greet(east, lat + 1)
        greet(west, lat + 1)

    for copy in flat:
        copy.wait()
    lane = lax.broadcasted_iota(jnp.int32, (height, breadth), 1)
    ocean = marine_ref[...].astype(jnp.float32)
    bands = []
    lane_band = lax.broadcasted_iota(jnp.int32, (BLK, breadth), 1) // BLK
    for jb in range(height // BLK):
        band = jnp.zeros((BLK, breadth), jnp.float32)
        for ib in range(breadth // BLK):
            band = jnp.where(lane_band == ib, kept_ref[jb, ib].astype(jnp.float32), band)
        bands.append(band)
    kept = jnp.concatenate(bands, axis=0)
    ext[0, PAD : PAD + height, 0:breadth] = ocean
    ext[1, PAD : PAD + height, 0:breadth] = depth_ref[...] * (ocean * kept)
    ext[2, PAD : PAD + height, 0:breadth] = elev_ref[...]

    lane_q = lax.broadcasted_iota(jnp.int32, (QROWS, breadth), 1)
    even_q = lax.rem(lane_q, 2) == 0
    for q in range(quarters):
        for copy in loads[q]:
            copy.wait()
        r0 = q * QROWS

        def level_step(l, carry, r0=r0, q=q):
            even, odd, su, sv, sp = carry
            weight = (levels - l).astype(jnp.float32) * (1.0 / levels)
            x = [held[f, l, r0 : r0 + QROWS, :] for f in range(NF)]
            for f in range(NF):
                k = NF * l + f
                turned = pltpu.roll(x[f], k, 1)
                before = jnp.where(k == 0, breadth - 1, k - 1)
                here = (lane_q == k) | (lane_q == before)
                if f % 2 == 0:
                    even = jnp.where(here, turned, even)
                else:
                    odd = jnp.where(here, turned, odd)
                if q == 0:
                    send_v[0, pl.ds(f * levels + l, 1), :] = held[f, l, 0:1, :]
                if q == quarters - 1:
                    send_v[1, pl.ds(f * levels + l, 1), :] = held[f, l, height - 1 : height, :]
            su = su + x[0]
            sv = sv + x[1]
            sp = sp + weight * (haline * x[3] - thermal * x[2])
            return even, odd, su, sv, sp

        zero = jnp.zeros((QROWS, breadth), jnp.float32)
        even, odd, su, sv, sp = lax.fori_loop(0, levels, level_step, (zero,) * 5, unroll=2)
        mask = ext[0, PAD + r0 : PAD + r0 + QROWS, 0:breadth]
        head = jnp.where(even_q, even, odd) * mask[:, 0:1]
        tail = jnp.where(even_q, odd, even) * mask[:, breadth - 1 : breadth]
        send_w[0, r0 : r0 + QROWS, :] = head
        send_e[0, r0 : r0 + QROWS, :] = tail
        inv = 1.0 / levels
        ext[3, PAD + r0 : PAD + r0 + QROWS, 0:breadth] = su * inv * mask
        ext[4, PAD + r0 : PAD + r0 + QROWS, 0:breadth] = sv * inv * mask
        ext[5, PAD + r0 : PAD + r0 + QROWS, 0:breadth] = sp * mask

    packed = jnp.zeros((height, breadth), jnp.float32)
    for a in range(NA):
        x = ext[a, PAD : PAD + height, 0:breadth]
        packed = jnp.where(lane // STRIP == a, roll(x, STRIP * a + S8, 1), packed)
        n3 = NF * levels + S8 * a
        send_v[0, n3 : n3 + S8, :] = x[0:S8, :]
        send_v[1, n3 : n3 + S8, :] = x[height - S8 : height, :]
    send_e[1] = packed
    send_w[1] = packed
    for f in range(NF):
        send_v[0, f * levels : (f + 1) * levels, :] *= ocean[0:1, :]
        send_v[1, f * levels : (f + 1) * levels, :] *= ocean[height - 1 : height, :]

    count = (
        (n_lon - 1) + (n_lat - 1)
        + 2 * (lat > 0).astype(jnp.int32) + 2 * (lat < n_lat - 1).astype(jnp.int32)
    )
    pl.semaphore_wait(barrier, count)

    def remote(src, dst, number, recv_number, a, b):
        return pltpu.make_async_remote_copy(
            src_ref=src, dst_ref=dst,
            send_sem=send_sem.at[number], recv_sem=recv_sem.at[recv_number],
            device_id={"lon": a, "lat": b}, device_id_type=pl.DeviceIdType.MESH,
        )

    up_slot = jnp.where(last, 1, 0)
    up_lat = jnp.where(last, lat, lat + 1)
    up_lon = jnp.where(last, mirror, lon)
    up_e = jnp.where(last, lax.rem(mirror + 1, n_lon), west)
    up_w = jnp.where(last, lax.rem(mirror + n_lon - 1, n_lon), east)
    top = send_e.at[1, pl.ds(height - S8, S8), :]
    bottom = send_e.at[1, pl.ds(0, S8), :]
    go_up = remote(send_v.at[1], recv_v.at[up_slot], 2, 2 + up_slot, up_lon, up_lat)
    go_e = remote(send_e, recv_w, 0, 0, east, lat)
    go_w = remote(send_w, recv_e, 1, 1, west, lat)
    go_up_e = remote(top, recv_c.at[up_slot, 0], 4, 4 + 2 * up_slot, up_e, up_lat)
    go_up_w = remote(top, recv_c.at[up_slot, 1], 5, 5 + 2 * up_slot, up_w, up_lat)
    down_lat = jnp.where(lat > 0, lat - 1, lat + 1)
    go_down = remote(send_v.at[0], recv_v.at[1], 3, 3, lon, down_lat)
    go_down_e = remote(bottom, recv_c.at[1, 0], 6, 6, west, down_lat)
    go_down_w = remote(bottom, recv_c.at[1, 1], 7, 7, east, down_lat)
    self_e = last & (up_e == lon)
    self_w = last & (up_w == lon)
    go_up.start()
    go_e.start()
    go_w.start()

    @pl.when(lat > 0)
    def _():
        go_down.start()
        go_down_e.start()
        go_down_w.start()

    @pl.when(jnp.logical_not(self_e))
    def _():
        go_up_e.start()

    @pl.when(jnp.logical_not(self_w))
    def _():
        go_up_w.start()

    @pl.when(self_e)
    def _():
        recv_c[1, 0] = send_e[1, height - S8 : height, :]

    @pl.when(self_w)
    def _():
        recv_c[1, 1] = send_e[1, height - S8 : height, :]

    def arrive(dst, recv_number):
        remote(dst, dst, 0, recv_number, east, lat).wait_recv()

    arrive(recv_w, 0)
    arrive(recv_e, 1)
    arrive(recv_v.at[1], 3)

    @pl.when(jnp.logical_not(self_e))
    def _():
        arrive(recv_c.at[1, 0], 6)

    @pl.when(jnp.logical_not(self_w))
    def _():
        arrive(recv_c.at[1, 1], 7)

    @pl.when(lat > 0)
    def _():
        arrive(recv_v.at[0], 2)
        arrive(recv_c.at[0, 0], 4)
        arrive(recv_c.at[0, 1], 5)

    @pl.when(lat == 0)
    def _():
        recv_v[0] = jnp.zeros(recv_v.shape[1:], jnp.float32)
        recv_c[0] = jnp.zeros(recv_c.shape[1:], jnp.float32)

    even_lane = lax.rem(lane, 2) == 0
    edge_ref[0] = jnp.where(even_lane, recv_e[0], recv_w[0])
    edge_ref[1] = jnp.where(even_lane, recv_w[0], recv_e[0])
    for f in range(NF):
        rows_ref[0, f] = recv_v[0, f * levels : (f + 1) * levels, :]
        top_rows = recv_v[1, f * levels : (f + 1) * levels, :]
        turned = reverse_lanes(top_rows)
        rows_ref[1, f] = jnp.where(last, -turned if f < 2 else turned, top_rows)

    strip_e = lax.rem(lane, STRIP) >= S8
    halo_lane = (lane < S8) | (lane >= breadth - S8)
    side = jnp.where(strip_e, recv_e[1], recv_w[1])
    c_lane = lax.broadcasted_iota(jnp.int32, (S8, breadth), 1)
    c_strip_e = lax.rem(c_lane, STRIP) >= S8
    c_halo = (c_lane < S8) | (c_lane >= breadth - S8)
    corner = [jnp.where(c_strip_e, recv_c[j, 0], recv_c[j, 1]) for j in range(2)]
    end = PAD + height
    for a in range(NA):
        fill = 1.0 if a == 2 else 0.0
        shift = -(STRIP * a + S8)
        ext[a, PAD:end, breadth : 2 * breadth] = jnp.where(halo_lane, roll(side, shift, 1), fill)
        n3 = NF * levels + S8 * a
        s_mid = recv_v[0, n3 : n3 + S8, :]
        s_out = jnp.where(c_halo, roll(corner[0], shift, 1), fill)
        if a == 2:
            s_mid = jnp.where(lat == 0, 1.0, s_mid)
            s_out = jnp.where(lat == 0, 1.0, s_out)
        ext[a, 0:PAD, 0:breadth] = s_mid
        ext[a, 0:PAD, breadth : 2 * breadth] = s_out
        sign = -1.0 if a in (3, 4) else 1.0
        n_mid = recv_v[1, n3 : n3 + S8, :]
        n_out = jnp.where(c_halo, roll(corner[1], shift, 1), fill)
        for at, block in ((0, n_mid), (breadth, n_out)):
            turned = sign * reverse_lanes(block)
            turned = jnp.concatenate([turned[i : i + 1] for i in range(S8 - 1, -1, -1)], axis=0)
            ext[a, end : end + PAD, at : at + breadth] = jnp.where(last, turned, block)

    rows = lax.broadcasted_iota(jnp.int32, (height + 2 * PAD, 2 * breadth), 0) + (lat * height - PAD)
    total_rows = n_lat * height
    rows = jnp.where(rows >= total_rows, 2 * total_rows - 1 - rows, rows)
    coriolis = 2.0 * (rows.astype(jnp.float32) + 0.5) / total_rows - 1.0
    ocean_x, column, um, vm, pm = ext[0], ext[1], ext[3], ext[4], ext[5]
    nu, nv, np_ = near(um), near(vm), near(pm)
    u_mean = ocean_x * (
        um + time_step * (
            coriolis * vm - 0.5 * (np_[0] - np_[1])
            + viscosity * (nu[0] + nu[1] + nu[2] + nu[3] - 4.0 * um)
        )
    )
    v_mean = ocean_x * (
        vm + time_step * (
            -coriolis * um - 0.5 * (np_[2] - np_[3])
            + viscosity * (nv[0] + nv[1] + nv[2] + nv[3] - 4.0 * vm)
        )
    )
    is_open = column > 0.0
    nc = near(column)
    weights = [0.5 * (column + c) for c in nc]
    diag = ext[2] + weights[0] + weights[1] + weights[2] + weights[3]
    scale = jnp.where(is_open, 1.0 / diag, 0.0)
    rhs = (-0.5 * source_gain) * (
        roll(u_mean, -1, 1) - roll(u_mean, 1, 1) + roll(v_mean, -1, 0) - roll(v_mean, 1, 0)
    )
    basis = [scale * rhs]
    for _ in range(ITERS):
        ny = near(basis[-1])
        total = weights[0] * ny[0] + weights[1] * ny[1] + weights[2] * ny[2] + weights[3] * ny[3]
        basis.append(scale * total)
    inner = [y[PAD:end, 0:breadth] for y in basis]
    weight_in = diag[PAD:end, 0:breadth]
    weighted = [weight_in * y for y in inner]
    moments = []
    for m in range(2 * ITERS):
        moments.append(jnp.sum(inner[m // 2] * weighted[(m + 1) // 2], axis=0, keepdims=True))
    while len(moments) < 8:
        moments.append(jnp.zeros((1, breadth), jnp.float32))
    tile = jnp.concatenate(moments, axis=0)

    def send_parts(tile, parts, me, n, sends, recvs, axis):
        parts[me] = tile
        copies = []
        for o in range(1, n):
            to = lax.rem(me + o, n)
            copy = pltpu.make_async_remote_copy(
                src_ref=parts.at[me], dst_ref=parts.at[me],
                send_sem=sends.at[o - 1], recv_sem=recvs.at[o - 1],
                device_id={axis: to}, device_id_type=pl.DeviceIdType.MESH,
            )
            copy.start()
            copies.append(copy)
        return copies

    def sum_parts(parts, me, n, sends, recvs, axis):
        for o in range(1, n):
            source = lax.rem(me + n - o, n)
            pltpu.make_async_remote_copy(
                src_ref=parts.at[source], dst_ref=parts.at[source],
                send_sem=sends.at[o - 1], recv_sem=recvs.at[o - 1],
                device_id={axis: source}, device_id_type=pl.DeviceIdType.MESH,
            ).wait_recv()
        total = parts[0]
        for i in range(1, n):
            total = total + parts[i]
        return total

    lon_copies = send_parts(tile, part_lon, lon, n_lon, lon_send, lon_recv, "lon")
    chunk = 8 if levels % 8 == 0 else 1
    chunks = levels // chunk
    mids = (u_mid, v_mid, t_mid, s_mid_)
    slope[...] = jnp.zeros_like(slope)
    lane8 = lax.broadcasted_iota(jnp.int32, (8, breadth), 1)
    first_lane, last_lane = lane8 == 0, lane8 == breadth - 1
    row8 = lax.broadcasted_iota(jnp.int32, (8, breadth), 0)
    mul_q = (time_step * viscosity,) * 2 + (time_step * diffusivity,) * 2

    def update_step(l, carry):
        b = lax.rem(l, 2)
        for f in range(NF):
            padded[b, f, PAD - 1 : PAD, :] = rows_ref[0, f, pl.ds(l, 1), :]
            padded[b, f, PAD + height : PAD + height + 1, :] = rows_ref[1, f, pl.ds(l, 1), :]
            for g in range(height // 8):
                mask = marine_ref[8 * g : 8 * g + 8, :].astype(jnp.float32)
                padded[b, f, PAD + 8 * g : PAD + 8 * g + 8, :] = held[f, l, 8 * g : 8 * g + 8, :] * mask
        for g in range(height // 8):
            r = 8 * g
            mask = marine_ref[r : r + 8, :].astype(jnp.float32)
            coriolis = (
                2.0 * ((row8 + (lat * height + r)).astype(jnp.float32) + 0.5) / total_rows - 1.0
            ) * time_step
            x, e, w, n, s = [], [], [], [], []
            for f in range(NF):
                at = PAD + r
                here = padded[b, f, at : at + 8, :]
                k = NF * l + f
                halo = pltpu.roll(
                    edge_ref[f % 2, r : r + 8, :], jnp.where(k == 0, 0, breadth - k), 1
                )
                x.append(here)
                e.append(pltpu.roll(jnp.where(first_lane, halo, here), breadth - 1, 1))
                w.append(pltpu.roll(jnp.where(last_lane, halo, here), 1, 1))
                n.append(padded[b, f, at + 1 : at + 9, :])
                s.append(padded[b, f, at - 1 : at + 7, :])
            gx = slope[0, r : r + 8, :] + (haline * (e[3] - w[3]) - thermal * (e[2] - w[2]))
            gy = slope[1, r : r + 8, :] + (haline * (n[3] - s[3]) - thermal * (n[2] - s[2]))
            slope[0, r : r + 8, :] = gx
            slope[1, r : r + 8, :] = gy
            new = [
                x[f] + mul_q[f] * (e[f] + w[f] + n[f] + s[f] - 4.0 * x[f]) for f in range(NF)
            ]
            new[0] = new[0] + (coriolis * x[1] - (0.5 * time_step) * gx)
            new[1] = new[1] - (coriolis * x[0] + (0.5 * time_step) * gy)
            for f in (2, 3):
                flux = e[0] * e[f] - w[0] * w[f] + n[1] * n[f] - s[1] * s[f]
                new[f] = new[f] - (0.5 * time_step) * flux
            for f in range(NF):
                done[f, l, r : r + 8, :] = mask * new[f]
        return carry

    stores = []

    def update(low, high):
        for c in range(low, high):
            lax.fori_loop(c * chunk, (c + 1) * chunk, update_step, 0)
            part = pl.ds(c * chunk, chunk)
            for f in range(NF):
                copy = pltpu.make_async_copy(
                    done.at[f, part], mids[f].at[part], store_sem.at[c, f]
                )
                copy.start()
                stores.append(copy)

    update(0, chunks // 2)
    tile = sum_parts(part_lon, lon, n_lon, lon_send, lon_recv, "lon")
    lat_copies = send_parts(tile, part_lat, lat, n_lat, lat_send, lat_recv, "lat")
    update(chunks // 2, chunks)
    tile = sum_parts(part_lat, lat, n_lat, lat_send, lat_recv, "lat")
    sums = jnp.broadcast_to(jnp.sum(tile, axis=1, keepdims=True), tile.shape)
    m = [sums[i : i + 1, :] for i in range(2 * ITERS)]

    def dot(a, b):
        total = 0.0
        for i, p in enumerate(a):
            for j, q in enumerate(b):
                total = total + (p * q) * m[i + j]
        return total

    one = jnp.ones((1, breadth), jnp.float32)
    z, d = [one], [one]
    x = []
    rz = m[0]
    for step in range(ITERS):
        image = [d[0]] + [d[i] - d[i - 1] for i in range(1, len(d))] + [-d[-1]]
        alpha = rz / dot(d, image)
        x = [alpha * d[i] + (x[i] if i < len(x) else 0.0) for i in range(len(d))]
        z = [(z[i] if i < len(z) else 0.0) - alpha * image[i] for i in range(len(image))]
        if step + 1 < ITERS:
            rz_new = dot(z, z)
            beta = rz_new / rz
            d = [z[i] + (beta * d[i] if i < len(d) else 0.0) for i in range(len(z))]
            rz = rz_new
    answer = x[0] * inner[0]
    for i in range(1, ITERS):
        answer = answer + x[i] * inner[i]
    left = z[0] * weighted[0]
    for i in range(1, ITERS + 1):
        left = left + z[i] * weighted[i]
    sol_ref[...] = answer
    res_ref[...] = left

    go_up.wait_send()
    go_e.wait_send()
    go_w.wait_send()

    @pl.when(lat > 0)
    def _():
        go_down.wait_send()
        go_down_e.wait_send()
        go_down_w.wait_send()

    @pl.when(jnp.logical_not(self_e))
    def _():
        go_up_e.wait_send()

    @pl.when(jnp.logical_not(self_w))
    def _():
        go_up_w.wait_send()

    for copy in lon_copies + lat_copies:
        copy.wait_send()
    for copy in stores:
        copy.wait()


def place_kernel(*refs):
    *arrays, sem = refs
    half = len(arrays) // 2
    copies = [
        pltpu.make_async_copy(arrays[i], arrays[half + i], sem.at[i]) for i in range(half)
    ]
    for copy in copies:
        copy.start()
    for copy in copies:
        copy.wait()


def local(
    zonal_current, meridional_current, warmth_anomaly, brine_anomaly,
    marine_indicator, retained_tile_indicator, seabed_thickness, elevation_pivot_entry,
):
    levels, height, breadth = zonal_current.shape
    n_lon, n_lat = lax.axis_size("lon"), lax.axis_size("lat")
    f32 = jnp.float32
    vmem = pl.BlockSpec(memory_space=pltpu.VMEM)
    hbm = pl.BlockSpec(memory_space=pltpu.HBM)
    chunk = 8 if levels % 8 == 0 else 1
    quarters = height // QROWS
    wide = NF * levels + NA * S8
    dma = pltpu.SemaphoreType.DMA
    fields = (zonal_current, meridional_current, warmth_anomaly, brine_anomaly)
    results = tuple(jax.ShapeDtypeStruct(x.shape, f32) for x in (*fields, seabed_thickness, seabed_thickness))
    middle = pl.pallas_call(
        surface_kernel,
        out_shape=results,
        in_specs=[hbm] * 8,
        out_specs=(hbm,) * 4 + (vmem,) * 2,
        scratch_shapes=[
            pltpu.VMEM((2, height, breadth), f32),
            pltpu.VMEM((2, NF, levels, breadth), f32),
            pltpu.VMEM((NF, levels, height, breadth), f32),
            pltpu.VMEM((2, NF, height + 2 * PAD, breadth), f32),
            pltpu.VMEM((2, height, breadth), f32),
            dma((levels // chunk, NF)),
            pltpu.VMEM((NF, levels, height, breadth), f32),
            pltpu.VMEM((2, height, breadth), f32),
            pltpu.VMEM((2, height, breadth), f32),
            pltpu.VMEM((2, wide, breadth), f32),
            pltpu.VMEM((2, height, breadth), f32),
            pltpu.VMEM((2, height, breadth), f32),
            pltpu.VMEM((2, wide, breadth), f32),
            pltpu.VMEM((2, 2, S8, breadth), f32),
            pltpu.VMEM((NA, height + 2 * PAD, 2 * breadth), f32),
            pltpu.VMEM((n_lon, 8, breadth), f32),
            pltpu.VMEM((n_lat, 8, breadth), f32),
            pltpu.VMEM((height, breadth), jnp.int32),
            pltpu.SMEM(retained_tile_indicator.shape, jnp.int32),
            pltpu.VMEM((height, breadth), f32),
            pltpu.VMEM((height, breadth), f32),
            dma((4,)),
            dma((quarters, NF)),
            dma((8,)),
            dma((8,)),
            dma((n_lon - 1,)),
            dma((n_lon - 1,)),
            dma((n_lat - 1,)),
            dma((n_lat - 1,)),
        ],
        compiler_params=pltpu.CompilerParams(
            collective_id=0, has_side_effects=True, vmem_limit_bytes=60 * 2**20
        ),
        name="surface",
    )(*fields, marine_indicator, retained_tile_indicator, seabed_thickness, elevation_pivot_entry)
    return pl.pallas_call(
        place_kernel,
        out_shape=results,
        in_specs=[hbm] * 6,
        out_specs=(hbm,) * 6,
        scratch_shapes=[dma((6,))],
        compiler_params=pltpu.CompilerParams(vmem_limit_bytes=60 * 2**20),
        name="place",
    )(*middle)


def solution(mesh):
    cube, flat = P(None, "lat", "lon"), P("lat", "lon")
    return jax.shard_map(
        local,
        mesh=mesh,
        in_specs=(cube,) * 4 + (flat,) * 4,
        out_specs=(cube,) * 4 + (flat,) * 2,
        check_vma=False,
    )
```

```python
import functools

import jax
import jax.numpy as jnp
from jax import lax
from jax.experimental import pallas as pl
from jax.experimental.pallas import tpu as pltpu
from jax.sharding import PartitionSpec as P

BLK = 16
ITERS = 3

time_step = 0.1
viscosity = 0.2
diffusivity = 0.15
thermal = 0.2
haline = 0.8
source_gain = 8.0

NF = 4
NA = 6
STRIP = 16
S8 = 8
QROWS = 32
PAD = 8


def reverse_lanes(x):
    index = x.shape[-1] - 1 - lax.broadcasted_iota(jnp.int32, x.shape, x.ndim - 1)
    return jnp.take_along_axis(x, index, axis=x.ndim - 1, mode="promise_in_bounds")


def roll(x, shift, axis):
    return pltpu.roll(x, shift % x.shape[axis], axis)


def near(x):
    return roll(x, -1, 1), roll(x, 1, 1), roll(x, -1, 0), roll(x, 1, 0)


def surface_kernel(
    u_ref, v_ref, t_ref, s_ref, marine_hbm, kept_hbm, depth_hbm, elev_hbm,
    u_mid, v_mid, t_mid, s_mid_, sol_ref, res_ref,
    edge_ref, rows_ref, done, padded, slope, store_sem, held, send_e, send_w, send_v, recv_e, recv_w, recv_v, recv_c, ext,
    part_lon, part_lat, marine_ref, kept_ref, depth_ref, elev_ref, flat_sem, load_sem, send_sem, recv_sem, lon_send, lon_recv, lat_send, lat_recv,
):
    n_lon, n_lat = lax.axis_size("lon"), lax.axis_size("lat")
    lon, lat = lax.axis_index("lon"), lax.axis_index("lat")
    levels, height, breadth = u_ref.shape
    last = lat == n_lat - 1
    east, west = lax.rem(lon + 1, n_lon), lax.rem(lon + n_lon - 1, n_lon)
    mirror = n_lon - 1 - lon

    flat = [
        pltpu.make_async_copy(src, dst, flat_sem.at[i])
        for i, (src, dst) in enumerate(
            ((marine_hbm, marine_ref), (kept_hbm, kept_ref), (depth_hbm, depth_ref), (elev_hbm, elev_ref))
        )
    ]
    for copy in flat:
        copy.start()
    fields = (u_ref, v_ref, t_ref, s_ref)
    quarters = height // QROWS
    loads = []
    for q in range(quarters):
        row = []
        for f in range(NF):
            copy = pltpu.make_async_copy(
                fields[f].at[:, pl.ds(q * QROWS, QROWS), :],
                held.at[f, :, pl.ds(q * QROWS, QROWS), :],
                load_sem.at[q, f],
            )
            copy.start()
            row.append(copy)
        loads.append(row)

    barrier = pltpu.get_barrier_semaphore()

    def greet(a, b):
        pl.semaphore_signal(
            barrier, inc=1, device_id={"lon": a, "lat": b}, device_id_type=pl.DeviceIdType.MESH
        )

    for o in range(1, n_lon):
        greet(lax.rem(lon + o, n_lon), lat)
    for o in range(1, n_lat):
        greet(lon, lax.rem(lat + o, n_lat))

    @pl.when(lat > 0)
    def _():
        greet(east, lat - 1)
        greet(west, lat - 1)

    @pl.when(lat < n_lat - 1)
    def _():
        greet(east, lat + 1)
        greet(west, lat + 1)

    for copy in flat:
        copy.wait()
    lane = lax.broadcasted_iota(jnp.int32, (height, breadth), 1)
    ocean = marine_ref[...].astype(jnp.float32)
    bands = []
    lane_band = lax.broadcasted_iota(jnp.int32, (BLK, breadth), 1) // BLK
    for jb in range(height // BLK):
        band = jnp.zeros((BLK, breadth), jnp.float32)
        for ib in range(breadth // BLK):
            band = jnp.where(lane_band == ib, kept_ref[jb, ib].astype(jnp.float32), band)
        bands.append(band)
    kept = jnp.concatenate(bands, axis=0)
    ext[0, PAD : PAD + height, 0:breadth] = ocean
    ext[1, PAD : PAD + height, 0:breadth] = depth_ref[...] * (ocean * kept)
    ext[2, PAD : PAD + height, 0:breadth] = elev_ref[...]

    lane_q = lax.broadcasted_iota(jnp.int32, (QROWS, breadth), 1)
    even_q = lax.rem(lane_q, 2) == 0
    for q in range(quarters):
        for copy in loads[q]:
            copy.wait()
        r0 = q * QROWS

        def level_step(l, carry, r0=r0, q=q):
            even, odd, su, sv, sp = carry
            weight = (levels - l).astype(jnp.float32) * (1.0 / levels)
            x = [held[f, l, r0 : r0 + QROWS, :] for f in range(NF)]
            for f in range(NF):
                k = NF * l + f
                turned = pltpu.roll(x[f], k, 1)
                before = jnp.where(k == 0, breadth - 1, k - 1)
                here = (lane_q == k) | (lane_q == before)
                if f % 2 == 0:
                    even = jnp.where(here, turned, even)
                else:
                    odd = jnp.where(here, turned, odd)
                if q == 0:
                    send_v[0, pl.ds(f * levels + l, 1), :] = held[f, l, 0:1, :]
                if q == quarters - 1:
                    send_v[1, pl.ds(f * levels + l, 1), :] = held[f, l, height - 1 : height, :]
            su = su + x[0]
            sv = sv + x[1]
            sp = sp + weight * (haline * x[3] - thermal * x[2])
            return even, odd, su, sv, sp

        zero = jnp.zeros((QROWS, breadth), jnp.float32)
        even, odd, su, sv, sp = lax.fori_loop(0, levels, level_step, (zero,) * 5, unroll=2)
        mask = ext[0, PAD + r0 : PAD + r0 + QROWS, 0:breadth]
        head = jnp.where(even_q, even, odd) * mask[:, 0:1]
        tail = jnp.where(even_q, odd, even) * mask[:, breadth - 1 : breadth]
        send_w[0, r0 : r0 + QROWS, :] = head
        send_e[0, r0 : r0 + QROWS, :] = tail
        inv = 1.0 / levels
        ext[3, PAD + r0 : PAD + r0 + QROWS, 0:breadth] = su * inv * mask
        ext[4, PAD + r0 : PAD + r0 + QROWS, 0:breadth] = sv * inv * mask
        ext[5, PAD + r0 : PAD + r0 + QROWS, 0:breadth] = sp * mask

    packed = jnp.zeros((height, breadth), jnp.float32)
    for a in range(NA):
        x = ext[a, PAD : PAD + height, 0:breadth]
        packed = jnp.where(lane // STRIP == a, roll(x, STRIP * a + S8, 1), packed)
        n3 = NF * levels + S8 * a
        send_v[0, n3 : n3 + S8, :] = x[0:S8, :]
        send_v[1, n3 : n3 + S8, :] = x[height - S8 : height, :]
    send_e[1] = packed
    send_w[1] = packed
    for f in range(NF):
        send_v[0, f * levels : (f + 1) * levels, :] *= ocean[0:1, :]
        send_v[1, f * levels : (f + 1) * levels, :] *= ocean[height - 1 : height, :]

    count = (
        (n_lon - 1) + (n_lat - 1)
        + 2 * (lat > 0).astype(jnp.int32) + 2 * (lat < n_lat - 1).astype(jnp.int32)
    )
    pl.semaphore_wait(barrier, count)

    def remote(src, dst, number, recv_number, a, b):
        return pltpu.make_async_remote_copy(
            src_ref=src, dst_ref=dst,
            send_sem=send_sem.at[number], recv_sem=recv_sem.at[recv_number],
            device_id={"lon": a, "lat": b}, device_id_type=pl.DeviceIdType.MESH,
        )

    up_slot = jnp.where(last, 1, 0)
    up_lat = jnp.where(last, lat, lat + 1)
    up_lon = jnp.where(last, mirror, lon)
    up_e = jnp.where(last, lax.rem(mirror + 1, n_lon), west)
    up_w = jnp.where(last, lax.rem(mirror + n_lon - 1, n_lon), east)
    top = send_e.at[1, pl.ds(height - S8, S8), :]
    bottom = send_e.at[1, pl.ds(0, S8), :]
    go_up = remote(send_v.at[1], recv_v.at[up_slot], 2, 2 + up_slot, up_lon, up_lat)
    go_e = remote(send_e, recv_w, 0, 0, east, lat)
    go_w = remote(send_w, recv_e, 1, 1, west, lat)
    go_up_e = remote(top, recv_c.at[up_slot, 0], 4, 4 + 2 * up_slot, up_e, up_lat)
    go_up_w = remote(top, recv_c.at[up_slot, 1], 5, 5 + 2 * up_slot, up_w, up_lat)
    down_lat = jnp.where(lat > 0, lat - 1, lat + 1)
    go_down = remote(send_v.at[0], recv_v.at[1], 3, 3, lon, down_lat)
    go_down_e = remote(bottom, recv_c.at[1, 0], 6, 6, west, down_lat)
    go_down_w = remote(bottom, recv_c.at[1, 1], 7, 7, east, down_lat)
    self_e = last & (up_e == lon)
    self_w = last & (up_w == lon)
    go_up.start()
    go_e.start()
    go_w.start()

    @pl.when(lat > 0)
    def _():
        go_down.start()
        go_down_e.start()
        go_down_w.start()

    @pl.when(jnp.logical_not(self_e))
    def _():
        go_up_e.start()

    @pl.when(jnp.logical_not(self_w))
    def _():
        go_up_w.start()

    @pl.when(self_e)
    def _():
        recv_c[1, 0] = send_e[1, height - S8 : height, :]

    @pl.when(self_w)
    def _():
        recv_c[1, 1] = send_e[1, height - S8 : height, :]

    def arrive(dst, recv_number):
        remote(dst, dst, 0, recv_number, east, lat).wait_recv()

    arrive(recv_w, 0)
    arrive(recv_e, 1)
    arrive(recv_v.at[1], 3)

    @pl.when(jnp.logical_not(self_e))
    def _():
        arrive(recv_c.at[1, 0], 6)

    @pl.when(jnp.logical_not(self_w))
    def _():
        arrive(recv_c.at[1, 1], 7)

    @pl.when(lat > 0)
    def _():
        arrive(recv_v.at[0], 2)
        arrive(recv_c.at[0, 0], 4)
        arrive(recv_c.at[0, 1], 5)

    @pl.when(lat == 0)
    def _():
        recv_v[0] = jnp.zeros(recv_v.shape[1:], jnp.float32)
        recv_c[0] = jnp.zeros(recv_c.shape[1:], jnp.float32)

    even_lane = lax.rem(lane, 2) == 0
    edge_ref[0] = jnp.where(even_lane, recv_e[0], recv_w[0])
    edge_ref[1] = jnp.where(even_lane, recv_w[0], recv_e[0])
    for f in range(NF):
        rows_ref[0, f] = recv_v[0, f * levels : (f + 1) * levels, :]
        top_rows = recv_v[1, f * levels : (f + 1) * levels, :]
        turned = reverse_lanes(top_rows)
        rows_ref[1, f] = jnp.where(last, -turned if f < 2 else turned, top_rows)

    strip_e = lax.rem(lane, STRIP) >= S8
    halo_lane = (lane < S8) | (lane >= breadth - S8)
    side = jnp.where(strip_e, recv_e[1], recv_w[1])
    c_lane = lax.broadcasted_iota(jnp.int32, (S8, breadth), 1)
    c_strip_e = lax.rem(c_lane, STRIP) >= S8
    c_halo = (c_lane < S8) | (c_lane >= breadth - S8)
    corner = [jnp.where(c_strip_e, recv_c[j, 0], recv_c[j, 1]) for j in range(2)]
    end = PAD + height
    for a in range(NA):
        fill = 1.0 if a == 2 else 0.0
        shift = -(STRIP * a + S8)
        ext[a, PAD:end, breadth : 2 * breadth] = jnp.where(halo_lane, roll(side, shift, 1), fill)
        n3 = NF * levels + S8 * a
        s_mid = recv_v[0, n3 : n3 + S8, :]
        s_out = jnp.where(c_halo, roll(corner[0], shift, 1), fill)
        if a == 2:
            s_mid = jnp.where(lat == 0, 1.0, s_mid)
            s_out = jnp.where(lat == 0, 1.0, s_out)
        ext[a, 0:PAD, 0:breadth] = s_mid
        ext[a, 0:PAD, breadth : 2 * breadth] = s_out
        sign = -1.0 if a in (3, 4) else 1.0
        n_mid = recv_v[1, n3 : n3 + S8, :]
        n_out = jnp.where(c_halo, roll(corner[1], shift, 1), fill)
        for at, block in ((0, n_mid), (breadth, n_out)):
            turned = sign * reverse_lanes(block)
            turned = jnp.concatenate([turned[i : i + 1] for i in range(S8 - 1, -1, -1)], axis=0)
            ext[a, end : end + PAD, at : at + breadth] = jnp.where(last, turned, block)

    rows = lax.broadcasted_iota(jnp.int32, (height + 2 * PAD, 2 * breadth), 0) + (lat * height - PAD)
    total_rows = n_lat * height
    rows = jnp.where(rows >= total_rows, 2 * total_rows - 1 - rows, rows)
    coriolis = 2.0 * (rows.astype(jnp.float32) + 0.5) / total_rows - 1.0
    ocean_x, column, um, vm, pm = ext[0], ext[1], ext[3], ext[4], ext[5]
    nu, nv, np_ = near(um), near(vm), near(pm)
    u_mean = ocean_x * (
        um + time_step * (
            coriolis * vm - 0.5 * (np_[0] - np_[1])
            + viscosity * (nu[0] + nu[1] + nu[2] + nu[3] - 4.0 * um)
        )
    )
    v_mean = ocean_x * (
        vm + time_step * (
            -coriolis * um - 0.5 * (np_[2] - np_[3])
            + viscosity * (nv[0] + nv[1] + nv[2] + nv[3] - 4.0 * vm)
        )
    )
    is_open = column > 0.0
    nc = near(column)
    weights = [0.5 * (column + c) for c in nc]
    diag = ext[2] + weights[0] + weights[1] + weights[2] + weights[3]
    scale = jnp.where(is_open, 1.0 / diag, 0.0)
    rhs = (-0.5 * source_gain) * (
        roll(u_mean, -1, 1) - roll(u_mean, 1, 1) + roll(v_mean, -1, 0) - roll(v_mean, 1, 0)
    )
    basis = [scale * rhs]
    for _ in range(ITERS):
        ny = near(basis[-1])
        total = weights[0] * ny[0] + weights[1] * ny[1] + weights[2] * ny[2] + weights[3] * ny[3]
        basis.append(scale * total)
    inner = [y[PAD:end, 0:breadth] for y in basis]
    weight_in = diag[PAD:end, 0:breadth]
    weighted = [weight_in * y for y in inner]
    moments = []
    for m in range(2 * ITERS):
        moments.append(jnp.sum(inner[m // 2] * weighted[(m + 1) // 2], axis=0, keepdims=True))
    while len(moments) < 8:
        moments.append(jnp.zeros((1, breadth), jnp.float32))
    tile = jnp.concatenate(moments, axis=0)

    def send_parts(tile, parts, me, n, sends, recvs, axis):
        parts[me] = tile
        copies = []
        for o in range(1, n):
            to = lax.rem(me + o, n)
            copy = pltpu.make_async_remote_copy(
                src_ref=parts.at[me], dst_ref=parts.at[me],
                send_sem=sends.at[o - 1], recv_sem=recvs.at[o - 1],
                device_id={axis: to}, device_id_type=pl.DeviceIdType.MESH,
            )
            copy.start()
            copies.append(copy)
        return copies

    def sum_parts(parts, me, n, sends, recvs, axis):
        for o in range(1, n):
            source = lax.rem(me + n - o, n)
            pltpu.make_async_remote_copy(
                src_ref=parts.at[source], dst_ref=parts.at[source],
                send_sem=sends.at[o - 1], recv_sem=recvs.at[o - 1],
                device_id={axis: source}, device_id_type=pl.DeviceIdType.MESH,
            ).wait_recv()
        total = parts[0]
        for i in range(1, n):
            total = total + parts[i]
        return total

    lon_copies = send_parts(tile, part_lon, lon, n_lon, lon_send, lon_recv, "lon")
    chunk = 8 if levels % 8 == 0 else 1
    chunks = levels // chunk
    mids = (u_mid, v_mid, t_mid, s_mid_)
    slope[...] = jnp.zeros_like(slope)
    lane8 = lax.broadcasted_iota(jnp.int32, (8, breadth), 1)
    first_lane, last_lane = lane8 == 0, lane8 == breadth - 1
    row8 = lax.broadcasted_iota(jnp.int32, (8, breadth), 0)
    mul_q = (time_step * viscosity,) * 2 + (time_step * diffusivity,) * 2

    def update_step(l, carry):
        b = lax.rem(l, 2)
        for f in range(NF):
            padded[b, f, PAD - 1 : PAD, :] = rows_ref[0, f, pl.ds(l, 1), :]
            padded[b, f, PAD + height : PAD + height + 1, :] = rows_ref[1, f, pl.ds(l, 1), :]
            for g in range(height // 8):
                mask = marine_ref[8 * g : 8 * g + 8, :].astype(jnp.float32)
                padded[b, f, PAD + 8 * g : PAD + 8 * g + 8, :] = held[f, l, 8 * g : 8 * g + 8, :] * mask
        for g in range(height // 8):
            r = 8 * g
            mask = marine_ref[r : r + 8, :].astype(jnp.float32)
            coriolis = (
                2.0 * ((row8 + (lat * height + r)).astype(jnp.float32) + 0.5) / total_rows - 1.0
            ) * time_step
            x, e, w, n, s = [], [], [], [], []
            for f in range(NF):
                at = PAD + r
                here = padded[b, f, at : at + 8, :]
                k = NF * l + f
                halo = pltpu.roll(
                    edge_ref[f % 2, r : r + 8, :], jnp.where(k == 0, 0, breadth - k), 1
                )
                x.append(here)
                e.append(pltpu.roll(jnp.where(first_lane, halo, here), breadth - 1, 1))
                w.append(pltpu.roll(jnp.where(last_lane, halo, here), 1, 1))
                n.append(padded[b, f, at + 1 : at + 9, :])
                s.append(padded[b, f, at - 1 : at + 7, :])
            gx = slope[0, r : r + 8, :] + (haline * (e[3] - w[3]) - thermal * (e[2] - w[2]))
            gy = slope[1, r : r + 8, :] + (haline * (n[3] - s[3]) - thermal * (n[2] - s[2]))
            slope[0, r : r + 8, :] = gx
            slope[1, r : r + 8, :] = gy
            new = [
                x[f] + mul_q[f] * (e[f] + w[f] + n[f] + s[f] - 4.0 * x[f]) for f in range(NF)
            ]
            new[0] = new[0] + (coriolis * x[1] - (0.5 * time_step) * gx)
            new[1] = new[1] - (coriolis * x[0] + (0.5 * time_step) * gy)
            for f in (2, 3):
                flux = e[0] * e[f] - w[0] * w[f] + n[1] * n[f] - s[1] * s[f]
                new[f] = new[f] - (0.5 * time_step) * flux
            for f in range(NF):
                done[f, l, r : r + 8, :] = mask * new[f]
        return carry

    stores = []

    def update(low, high):
        for c in range(low, high):
            lax.fori_loop(c * chunk, (c + 1) * chunk, update_step, 0)
            part = pl.ds(c * chunk, chunk)
            for f in range(NF):
                copy = pltpu.make_async_copy(
                    done.at[f, part], mids[f].at[part], store_sem.at[c, f]
                )
                copy.start()
                stores.append(copy)

    update(0, chunks // 2)
    tile = sum_parts(part_lon, lon, n_lon, lon_send, lon_recv, "lon")
    lat_copies = send_parts(tile, part_lat, lat, n_lat, lat_send, lat_recv, "lat")
    update(chunks // 2, chunks)
    tile = sum_parts(part_lat, lat, n_lat, lat_send, lat_recv, "lat")
    sums = jnp.broadcast_to(jnp.sum(tile, axis=1, keepdims=True), tile.shape)
    m = [sums[i : i + 1, :] for i in range(2 * ITERS)]

    def dot(a, b):
        total = 0.0
        for i, p in enumerate(a):
            for j, q in enumerate(b):
                total = total + (p * q) * m[i + j]
        return total

    one = jnp.ones((1, breadth), jnp.float32)
    z, d = [one], [one]
    x = []
    rz = m[0]
    for step in range(ITERS):
        image = [d[0]] + [d[i] - d[i - 1] for i in range(1, len(d))] + [-d[-1]]
        alpha = rz / dot(d, image)
        x = [alpha * d[i] + (x[i] if i < len(x) else 0.0) for i in range(len(d))]
        z = [(z[i] if i < len(z) else 0.0) - alpha * image[i] for i in range(len(image))]
        if step + 1 < ITERS:
            rz_new = dot(z, z)
            beta = rz_new / rz
            d = [z[i] + (beta * d[i] if i < len(d) else 0.0) for i in range(len(z))]
            rz = rz_new
    answer = x[0] * inner[0]
    for i in range(1, ITERS):
        answer = answer + x[i] * inner[i]
    left = z[0] * weighted[0]
    for i in range(1, ITERS + 1):
        left = left + z[i] * weighted[i]
    sol_ref[...] = answer
    res_ref[...] = left

    go_up.wait_send()
    go_e.wait_send()
    go_w.wait_send()

    @pl.when(lat > 0)
    def _():
        go_down.wait_send()
        go_down_e.wait_send()
        go_down_w.wait_send()

    @pl.when(jnp.logical_not(self_e))
    def _():
        go_up_e.wait_send()

    @pl.when(jnp.logical_not(self_w))
    def _():
        go_up_w.wait_send()

    for copy in lon_copies + lat_copies:
        copy.wait_send()
    for copy in stores:
        copy.wait()


def place_kernel(*refs):
    arrays, held, flat, load_sem, store_sem, flat_load, flat_store = refs[:12], *refs[12:]
    levels = arrays[0].shape[0]
    chunk = 8 if levels % 8 == 0 else 1
    moves = []
    for c in range(levels // chunk):
        part = pl.ds(c * chunk, chunk)
        for f in range(NF):
            slot = held.at[f, part]
            moves.append((
                pltpu.make_async_copy(arrays[f].at[part], slot, load_sem.at[c, f]),
                pltpu.make_async_copy(slot, arrays[6 + f].at[part], store_sem.at[c, f]),
            ))
    for i in range(2):
        moves.append((
            pltpu.make_async_copy(arrays[4 + i], flat.at[i], flat_load.at[i]),
            pltpu.make_async_copy(flat.at[i], arrays[10 + i], flat_store.at[i]),
        ))
    for load, _ in moves:
        load.start()
    for load, store in moves:
        load.wait()
        store.start()
    for _, store in moves:
        store.wait()


def local(
    zonal_current, meridional_current, warmth_anomaly, brine_anomaly,
    marine_indicator, retained_tile_indicator, seabed_thickness, elevation_pivot_entry,
):
    levels, height, breadth = zonal_current.shape
    n_lon, n_lat = lax.axis_size("lon"), lax.axis_size("lat")
    f32 = jnp.float32
    vmem = pl.BlockSpec(memory_space=pltpu.VMEM)
    hbm = pl.BlockSpec(memory_space=pltpu.HBM)
    chunk = 8 if levels % 8 == 0 else 1
    quarters = height // QROWS
    wide = NF * levels + NA * S8
    dma = pltpu.SemaphoreType.DMA
    fields = (zonal_current, meridional_current, warmth_anomaly, brine_anomaly)
    results = tuple(jax.ShapeDtypeStruct(x.shape, f32) for x in (*fields, seabed_thickness, seabed_thickness))
    middle = pl.pallas_call(
        surface_kernel,
        out_shape=results,
        in_specs=[hbm] * 8,
        out_specs=(hbm,) * 4 + (vmem,) * 2,
        scratch_shapes=[
            pltpu.VMEM((2, height, breadth), f32),
            pltpu.VMEM((2, NF, levels, breadth), f32),
            pltpu.VMEM((NF, levels, height, breadth), f32),
            pltpu.VMEM((2, NF, height + 2 * PAD, breadth), f32),
            pltpu.VMEM((2, height, breadth), f32),
            dma((levels // chunk, NF)),
            pltpu.VMEM((NF, levels, height, breadth), f32),
            pltpu.VMEM((2, height, breadth), f32),
            pltpu.VMEM((2, height, breadth), f32),
            pltpu.VMEM((2, wide, breadth), f32),
            pltpu.VMEM((2, height, breadth), f32),
            pltpu.VMEM((2, height, breadth), f32),
            pltpu.VMEM((2, wide, breadth), f32),
            pltpu.VMEM((2, 2, S8, breadth), f32),
            pltpu.VMEM((NA, height + 2 * PAD, 2 * breadth), f32),
            pltpu.VMEM((n_lon, 8, breadth), f32),
            pltpu.VMEM((n_lat, 8, breadth), f32),
            pltpu.VMEM((height, breadth), jnp.int32),
            pltpu.SMEM(retained_tile_indicator.shape, jnp.int32),
            pltpu.VMEM((height, breadth), f32),
            pltpu.VMEM((height, breadth), f32),
            dma((4,)),
            dma((quarters, NF)),
            dma((8,)),
            dma((8,)),
            dma((n_lon - 1,)),
            dma((n_lon - 1,)),
            dma((n_lat - 1,)),
            dma((n_lat - 1,)),
        ],
        compiler_params=pltpu.CompilerParams(
            collective_id=0, has_side_effects=True, vmem_limit_bytes=60 * 2**20
        ),
        name="surface",
    )(*fields, marine_indicator, retained_tile_indicator, seabed_thickness, elevation_pivot_entry)
    return pl.pallas_call(
        place_kernel,
        out_shape=results,
        in_specs=[hbm] * 6,
        out_specs=(hbm,) * 6,
        scratch_shapes=[
            pltpu.VMEM((NF, levels, height, breadth), f32),
            pltpu.VMEM((2, height, breadth), f32),
            dma((levels // chunk, NF)),
            dma((levels // chunk, NF)),
            dma((2,)),
            dma((2,)),
        ],
        compiler_params=pltpu.CompilerParams(vmem_limit_bytes=60 * 2**20),
        name="place",
    )(*middle)


def solution(mesh):
    cube, flat = P(None, "lat", "lon"), P("lat", "lon")
    return jax.shard_map(
        local,
        mesh=mesh,
        in_specs=(cube,) * 4 + (flat,) * 4,
        out_specs=(cube,) * 4 + (flat,) * 2,
        check_vma=False,
    )
```
